256 devices in a mesh: seq: 64 (over z, x, core), head: 4 (over y).
Axes of the slice: x: 4, y: 4, z: 8, core: 2. Of those that a mesh axis runs over, the one named last changes fastest.
Arguments:
- queries: bfloat16 [49152, 2048], P('seq', 'head'), may hold values from -6 to 6
- attn_keys: bfloat16 [49152, 2048], P('seq', 'head'), may hold values from -6 to 6
- attn_values: bfloat16 [49152, 2048], P('seq', 'head'), may hold values from -36 to 36
- out_weight: bfloat16 [2048, 2048], P('head'), may hold values from -0.125 to 0.125
- grad_out: bfloat16 [49152, 2048], P('seq', 'head'), may hold values from -6 to 6
- drop_seed: int32 [1], replicated, may hold values from 0 to 32748
Outputs:
- output: bfloat16 [49152, 2048], P('seq', 'head')
- grad_queries: bfloat16 [49152, 2048], P('seq', 'head')
- grad_keys: bfloat16 [49152, 2048], P('seq', 'head')
- grad_values: bfloat16 [49152, 2048], P('seq', 'head')
- grad_weight: bfloat16 [2048, 2048], P('head')
The draws below stay inside these ranges and needn't reach their ends.
All inputs are finite; a program needn't handle non-finite values.
Results may differ from the reference program's by a relative error of at most 0.023.
Values may be sent and summed in bfloat16 or wider, within the bound.
A program may use at most 128 MiB of HBM per device.

```python
import math
import jax
import jax.numpy as jnp
from jax import lax

D = 2048
HEADS = 16
HD = 128
SPAN = 256
TOKENS = 49152
N_HEAD = 4


def draw_attn_values(key, part):
    key = jax.random.fold_in(key, 11)
    key_base, key_rows, key_cols = jax.random.split(key, 3)
    row_scale = jnp.exp(jax.random.uniform(key_rows, (TOKENS, 1), jnp.float32, math.log(0.3), math.log(3.0)))
    col_scale = jnp.exp(jax.random.uniform(key_cols, (1, D), jnp.float32, math.log(0.3), math.log(3.0)))
    base = jnp.clip(jax.random.normal(key_base, (TOKENS, D), jnp.float32), -4.0, 4.0)
    values = base * row_scale * col_scale
    return values.astype(jnp.bfloat16)


def levels(stream_key, dims, cuts, least, high):
    def one(position, shards_of):
        steps = jax.random.uniform(jax.random.fold_in(jax.random.fold_in(stream_key, 6), position), (shards_of,), jnp.float32, least / len(cuts), high / len(cuts))
        return jnp.repeat(jnp.exp(steps), dims[position] // shards_of).reshape((-1,) + (1,) * (len(dims) - position - 1))

    gain = one(*cuts[0])
    for cut in cuts[1:]:
        gain = gain * one(*cut)
    return gain


def scatter_about(stream_key, extent, deviation, reach, pieces=(), kind=jnp.bfloat16):
    level = levels(stream_key, extent, pieces, -0.22, 0.18) if pieces else 1.0
    values = jax.random.normal(stream_key, extent, jnp.float32) * deviation * level
    return jnp.minimum(jnp.maximum(values, -reach), reach).astype(kind)


def setup_inputs(seed: int = 0) -> dict:
    keys = jax.random.split(jax.random.key(seed), 7)
    return {
        "queries": scatter_about(keys[0], (TOKENS, D), 1.0, 6.0, ((0, 64), (1, 4))),
        "attn_keys": scatter_about(keys[1], (TOKENS, D), 1.0, 6.0, ((0, 64), (1, 4))),
        "attn_values": draw_attn_values(jax.random.fold_in(keys[6], 71), 0),
        "out_weight": scatter_about(keys[3], (D, D), D ** -0.5, 0.125, ((0, 4),)),
        "grad_out": scatter_about(keys[4], (TOKENS, D), 1.0, 6.0, ((0, 64), (1, 4))),
        "drop_seed": jax.random.randint(keys[5], (1,), 0, 32749).astype(jnp.int32),
    }


eps_norm = 1e-05
keep_scale = 1.0 / 0.9

def keep_table(drop_seed, positions, features):
    seed_value = drop_seed[0].astype(jnp.int32)
    mixing = (positions * 181 + features * 227 + seed_value) % 32749
    hashed = (mixing * mixing % 32749 * 173 + mixing * 59 + features * 13 + positions * 7) % 32749
    return hashed % 10 != 0

def reference(queries, attn_keys, attn_values, out_weight, grad_out, drop_seed):
    tokens_all = queries.shape[0]
    n_blocks = tokens_all // SPAN

    def split(array):
        return array.reshape(n_blocks, SPAN, HEADS, HD)
    query_blocks = split(queries)
    key_blocks = split(attn_keys)
    value_blocks = split(attn_values)
    causal = jnp.tril(jnp.ones((SPAN, SPAN), dtype=bool))[None]

    def forward_step(state, block):
        query, key_block, value = block
        query_f = query.astype(jnp.float32)
        key_f = key_block.astype(jnp.float32)
        value_f = value.astype(jnp.float32)
        state_b16 = state.astype(jnp.bfloat16)
        inter = jnp.einsum('thi,hij->thj', query_f, state_b16.astype(jnp.float32))
        scores = jnp.einsum('thi,shi->hts', query_f, key_f)
        causal_scores = jnp.where(causal, scores, 0.0).astype(jnp.bfloat16)
        intra = jnp.einsum('hts,shj->thj', causal_scores.astype(jnp.float32), value_f)
        new_state = state + jnp.einsum('shi,shj->hij', key_f, value_f)
        return (new_state, (inter + intra, state_b16))
    zero_state = jnp.zeros((HEADS, HD, HD), jnp.float32)
    _, (mixed, states_b16) = lax.scan(forward_step, zero_state, (query_blocks, key_blocks, value_blocks))
    inv_rms = 1.0 / jnp.sqrt(lax.optimization_barrier(jnp.mean(mixed * mixed, axis=-1, keepdims=True)) + eps_norm)
    normed = (mixed * inv_rms).astype(jnp.bfloat16).reshape(tokens_all, D)
    group_width = D // N_HEAD
    projected = jnp.zeros((tokens_all, D), jnp.float32)
    for group in range(N_HEAD):
        lower = group * group_width
        upper = lower + group_width
        piece = jnp.dot(normed[:, lower:upper], out_weight[lower:upper], preferred_element_type=jnp.float32)
        projected = projected + lax.optimization_barrier(piece.astype(jnp.bfloat16)).astype(jnp.float32)
    positions = jnp.arange(tokens_all, dtype=jnp.int32)[:, None]
    features = jnp.arange(D, dtype=jnp.int32)[None, :]
    keep = keep_table(drop_seed, positions, features)
    output = jnp.where(keep, projected * keep_scale, 0.0).astype(jnp.bfloat16)
    grad_proj = jnp.where(keep, grad_out.astype(jnp.float32) * keep_scale, 0.0).astype(jnp.bfloat16)
    grad_normed = jnp.dot(grad_proj, out_weight.T, preferred_element_type=jnp.float32)
    weight_total = jnp.dot(normed.T, grad_proj, preferred_element_type=jnp.float32)
    grad_weight = (weight_total * (1.0 / math.sqrt(tokens_all))).astype(jnp.bfloat16)
    grad_blocks = grad_normed.reshape(n_blocks, SPAN, HEADS, HD)
    grad_mixed = (inv_rms * (grad_blocks - mixed * inv_rms * inv_rms * lax.optimization_barrier(jnp.mean(grad_blocks * mixed, axis=-1, keepdims=True)))).astype(jnp.bfloat16)

    def backward_step(carry, block):
        query, key_block, value, grad_block, state_b16 = block
        query_f = query.astype(jnp.float32)
        key_f = key_block.astype(jnp.float32)
        value_f = value.astype(jnp.float32)
        grad_f = grad_block.astype(jnp.float32)
        state_f = state_b16.astype(jnp.float32)
        suffix_f = carry.astype(jnp.bfloat16).astype(jnp.float32)
        scores = jnp.einsum('thi,shi->hts', query_f, key_f)
        causal_f = jnp.where(causal, scores, 0.0).astype(jnp.bfloat16).astype(jnp.float32)
        grad_sc = jnp.einsum('thj,shj->hts', grad_f, value_f)
        grad_sc = jnp.where(causal, grad_sc, 0.0).astype(jnp.bfloat16).astype(jnp.float32)
        grad_query = jnp.einsum('thj,hij->thi', grad_f, state_f) + jnp.einsum('hts,shi->thi', grad_sc, key_f)
        grad_key = jnp.einsum('shj,hij->shi', value_f, suffix_f) + jnp.einsum('hts,thi->shi', grad_sc, query_f)
        grad_value = jnp.einsum('shi,hij->shj', key_f, suffix_f) + jnp.einsum('hts,thj->shj', causal_f, grad_f)
        new_carry = carry + jnp.einsum('thi,thj->hij', query_f, grad_f)
        return (new_carry, (grad_query.astype(jnp.bfloat16), grad_key.astype(jnp.bfloat16), grad_value.astype(jnp.bfloat16)))
    _, (grad_q, grad_k, grad_v) = lax.scan(backward_step, zero_state, (query_blocks, key_blocks, value_blocks, grad_mixed, states_b16), reverse=True)
    return (output, grad_q.reshape(tokens_all, D), grad_k.reshape(tokens_all, D), grad_v.reshape(tokens_all, D), grad_weight)
```

```python
import functools
import math

import jax
import jax.numpy as jnp
import numpy as np
from jax import lax
from jax.experimental import pallas as pl
from jax.experimental.pallas import tpu as pltpu
from jax.sharding import PartitionSpec as P

HD = 128
SPAN = 256
ROWS = 768
WIDTH = 512
MODEL = 2048
BLOCKS = ROWS // SPAN
HEADS = WIDTH // HD
N_ROW = 8
N_Z = 8
N_X = 4
HALF = SPAN // 2
EPS = 1e-05
KEEP_SCALE = 1.0 / 0.9
MODULUS = 32749.0
INVERSE = float(np.float32((1.0 - 2.0**-22) / 32749.0))
GRAD_SCALE = 1.0 / math.sqrt(49152)
MESH = pl.DeviceIdType.MESH
F32 = jnp.float32
BF16 = jnp.bfloat16

NN = (((1,), (0,)), ((), ()))
NT = (((1,), (1,)), ((), ()))
TN = (((0,), (0,)), ((), ()))


def dot(a, b, dims=NN):
    return lax.dot_general(a, b, dims, preferred_element_type=F32)


def wrap(value):
    quotient = jnp.floor(value * INVERSE)
    rest = value - quotient * MODULUS
    return jnp.where(rest >= MODULUS, rest - MODULUS, rest)


def keep_scales(positions, features, seed):
    mixing = wrap((positions * 181 + seed).astype(F32) + (features * 227).astype(F32))
    whole = mixing.astype(jnp.int32)
    square = whole * whole
    quotient = jnp.floor(square.astype(F32) * INVERSE).astype(jnp.int32)
    rest = square - quotient * 32749
    rest = jnp.where(rest >= 32749, rest - 32749, rest).astype(F32)
    offsets = (positions * 7).astype(F32) + (features * 13).astype(F32)
    hashed = wrap(rest * 173.0 + mixing * 59.0 + offsets)
    tens = jnp.floor((hashed + 0.5) * 0.1)
    return jnp.where(hashed - tens * 10.0 != 0.0, KEEP_SCALE, 0.0).astype(F32)


def rows(block):
    return pl.ds(block * SPAN, SPAN)


def half_rows(block, half):
    return pl.ds(block * SPAN + half * HALF, HALF)


def head(h):
    return pl.ds(h * HD, HD)


def kernel(
    seed_ref, q_hbm, k_hbm, v_hbm, w_hbm, go_hbm,
    out_hbm, gq_hbm, gk_hbm, gv_hbm, gw_hbm,
    q, k, v, go, w, scale, gp, kv, cs, state, mixed, inv, normed, turned,
    ps, own, relay_in, rin, gn, gm, gkv, gk_acc, gv_acc, out_b, gq_b, gk_b, gv_b,
    f_sb, f_rb, f_zs, f_zb, f_pb, f_fb, b_sb, b_rb, b_zs, b_zb, b_pb, b_fb,
    wsend, wown, wrecv, xs, xb, zsw, zbw, zone, zg, xg, pg,
    load_sem, store_sem, ag_s, ag_r, agr_s, agr_r, rs_s, rs_r,
    scan_s, scan_r, core_s, core_r, wx_s, wx_r, wz_s, wz_r,
):
    seq = lax.axis_index("seq")
    y = lax.axis_index("head")
    z = seq // N_ROW
    r = seq % N_ROW
    x = r // 2
    c = r % 2
    other = 1 - c

    def at(zz, rr, yy):
        return {"seq": zz * N_ROW + rr, "head": yy}

    y_next, y_prev, y_far = (y + 1) % 4, (y + 3) % 4, (y + 2) % 4
    beside = (at(z, r, y_next), at(z, r, y_prev))
    partner = at(z, x * 2 + other, y)

    def row_peer(i):
        return (r + i) % N_ROW

    def z_peer(i):
        return (z + i) % N_Z

    def x_peer(i):
        return (x + i) % N_X

    def remote(src, dst, send, recv, device):
        return pltpu.make_async_remote_copy(
            src_ref=src, dst_ref=dst, send_sem=send, recv_sem=recv,
            device_id=device, device_id_type=MESH,
        )

    loads = [
        pltpu.make_async_copy(a, b, load_sem.at[i])
        for i, (a, b) in enumerate(
            ((go_hbm, go), (k_hbm, k), (v_hbm, v), (q_hbm, q), (w_hbm, w))
        )
    ]
    for load in loads:
        load.start()

    barrier = pltpu.get_barrier_semaphore()
    for device in beside:
        pl.semaphore_signal(barrier, inc=1, device_id=device, device_id_type=MESH)

    def greet(i, _):
        pl.semaphore_signal(
            barrier, inc=1, device_id=at(z, row_peer(i), y), device_id_type=MESH
        )
        pl.semaphore_signal(
            barrier, inc=1, device_id=at(z_peer(i), r, y), device_id_type=MESH
        )
        return 0

    lax.fori_loop(1, N_ROW, greet, 0)

    def ag_own(b, way):
        return remote(
            gp.at[0, rows(b)], gp.at[1 + way, rows(b)], ag_s.at[way, b], ag_r.at[way, b],
            beside[way],
        )

    def ag_relay(b, way):
        part = half_rows(b, way)
        return remote(
            gp.at[1 + way, part], gp.at[3, part], agr_s.at[way, b], agr_r.at[way, b],
            beside[way],
        )

    seed = seed_ref[0]
    first_row = seq * ROWS
    first_column = y * WIDTH
    features = first_column + lax.broadcasted_iota(jnp.int32, (1, WIDTH), 1)
    TILE = 16

    def mask(b):
        def step(i, _):
            start = pl.multiple_of(b * SPAN + i * TILE, TILE)
            positions = first_row + start + lax.broadcasted_iota(jnp.int32, (TILE, 1), 0)
            kept = keep_scales(positions, features, seed)
            at_rows = pl.ds(start, TILE)
            scale[at_rows, :] = kept
            gp[0, at_rows, :] = (go[at_rows, :].astype(F32) * kept).astype(BF16)
            return 0

        lax.fori_loop(0, SPAN // TILE, step, 0)

    loads[0].wait()
    mask(0)
    loads[1].wait()
    loads[2].wait()

    def block_states(b, _):
        at_rows = pl.ds(pl.multiple_of(b * SPAN, SPAN), SPAN)
        for h in range(HEADS):
            kv[b, h] = dot(k[at_rows, head(h)], v[at_rows, head(h)], TN)
        return 0

    lax.fori_loop(0, BLOCKS, block_states, 0)

    def fill(sb, parts):
        for h in range(HEADS):
            total = (parts[0, h] + parts[1, h] + parts[2, h]).astype(BF16)
            sb[2 * h] = total[: HD // 2]
            sb[2 * h + 1] = total[HD // 2 :]

    def scan_one(n, i, sb, rb):
        t = row_peer(i)
        return remote(sb.at[t], rb.at[r], scan_s.at[n, 0, i], scan_r.at[n, 0, i], at(z, t, y))

    def scan_two(n, i, zs, zb):
        t = z_peer(i)
        return remote(zs, zb.at[z], scan_s.at[n, 1, i], scan_r.at[n, 1, i], at(t, r, y))

    def scan_three(n, i, pb, fb):
        t = row_peer(i)
        return remote(pb.at[t], fb.at[r], scan_s.at[n, 2, i], scan_r.at[n, 2, i], at(z, t, y))

    def loop(count, act):
        def step(i, _):
            act(i)
            return 0

        lax.fori_loop(1, count, step, 0)

    def row_from(i):
        return (r + N_ROW - i) % N_ROW

    def z_from(i):
        return (z + N_Z - i) % N_Z

    def x_from(i):
        return (x + N_X - i) % N_X

    def scan_start(n, sb, rb):
        rb[r] = sb[r]
        loop(N_ROW, lambda i: scan_one(n, i, sb, rb).start())

    def scan_middle(n, rb, zs, zb):
        loop(
            N_ROW,
            lambda i: remote(
                rb.at[0], rb.at[row_from(i)], scan_s.at[n, 0, i], scan_r.at[n, 0, i], partner
            ).wait_recv(),
        )
        total = rb[0].astype(F32)
        for j in range(1, N_ROW):
            total = total + rb[j].astype(F32)
        total = total.astype(BF16)
        zs[...] = total
        zb[z] = total
        loop(N_Z, lambda i: scan_two(n, i, zs, zb).start())

    def scan_late(n, rb, zb, pb, fb, reverse):
        loop(
            N_Z,
            lambda i: remote(
                zb.at[0], zb.at[z_from(i)], scan_s.at[n, 1, i], scan_r.at[n, 1, i], partner
            ).wait_recv(),
        )
        run = jnp.zeros((HD // 2, HD), F32)
        for j in range(N_Z):
            wanted = (j > z) if reverse else (j < z)
            run = run + jnp.where(wanted, zb[j].astype(F32), 0.0)
        order = range(N_ROW - 1, -1, -1) if reverse else range(N_ROW)
        for j in order:
            pb[j] = run.astype(BF16)
            run = run + rb[j].astype(F32)
        fb[r] = pb[r]
        loop(N_ROW, lambda i: scan_three(n, i, pb, fb).start())

    def scan_end(n, fb):
        loop(
            N_ROW,
            lambda i: remote(
                fb.at[0], fb.at[row_from(i)], scan_s.at[n, 2, i], scan_r.at[n, 2, i], partner
            ).wait_recv(),
        )

    def scan_sent(n, sb, rb, zs, zb, pb, fb):
        loop(N_ROW, lambda i: scan_one(n, i, sb, rb).wait_send())
        loop(N_Z, lambda i: scan_two(n, i, zs, zb).wait_send())
        loop(N_ROW, lambda i: scan_three(n, i, pb, fb).wait_send())

    fill(f_sb, kv)
    pl.semaphore_wait(barrier, 2 + N_ROW - 1 + N_Z - 1)
    scan_start(0, f_sb, f_rb)
    for way in range(2):
        ag_own(0, way).start()
    for b in range(1, BLOCKS):
        mask(b)
        for way in range(2):
            ag_own(b, way).start()
    scan_middle(0, f_rb, f_zs, f_zb)

    loads[3].wait()
    causal = lax.broadcasted_iota(jnp.int32, (SPAN, SPAN), 0) >= lax.broadcasted_iota(
        jnp.int32, (SPAN, SPAN), 1
    )

    def scores(b, _):
        at_rows = pl.ds(pl.multiple_of(b * SPAN, SPAN), SPAN)
        for h in range(HEADS):
            value = dot(q[at_rows, head(h)], k[at_rows, head(h)], NT)
            value = jnp.where(causal, value, 0.0).astype(BF16)
            cs[b * HEADS + h] = value
            mixed[at_rows, head(h)] = dot(value, v[at_rows, head(h)])
        return 0

    lax.fori_loop(0, BLOCKS, scores, 0)
    scan_late(0, f_rb, f_zb, f_pb, f_fb, False)
    loads[4].wait()

    def columns(block):
        return pl.ds(pl.multiple_of(block * WIDTH, WIDTH), WIDTH)

    model_block = (y, y_prev, y_next, y_far)

    def grad_normed(slot, b):
        def go_on(b, _):
            at_rows = pl.ds(pl.multiple_of(b * SPAN, SPAN), SPAN)
            term = dot(gp[slot, at_rows, :], w[:, columns(model_block[slot])], NT)
            gn[at_rows, :] = term if slot == 0 else gn[at_rows, :] + term
            return 0

        lax.fori_loop(b, b + 1, go_on, 0) if b is not None else lax.fori_loop(
            0, BLOCKS, go_on, 0
        )

    grad_normed(0, None)
    for way in range(2):
        ag_own(0, way).wait_recv()
        ag_relay(0, way).start()
    scan_end(0, f_fb)

    def mix(b, _):
        at_rows = pl.ds(pl.multiple_of(b * SPAN, SPAN), SPAN)
        for h in range(HEADS):
            run = jnp.concatenate([f_fb[2 * h], f_fb[2 * h + 1]], axis=0).astype(F32)
            for earlier in range(BLOCKS - 1):
                run = run + jnp.where(earlier < b, kv[earlier, h], 0.0)
            held = run.astype(BF16)
            state[b * HEADS + h] = held
            value = mixed[at_rows, head(h)] + dot(q[at_rows, head(h)], held)
            mixed[at_rows, head(h)] = value
            power = jnp.sum(value * value, axis=1, keepdims=True) * (1.0 / HD)
            inverse = lax.rsqrt(power + EPS)
            inv[at_rows, head(h)] = jnp.broadcast_to(inverse, (SPAN, HD))
            normed[at_rows, head(h)] = (value * inverse).astype(BF16)
        turned[:, at_rows] = normed[at_rows, :].T
        return 0

    lax.fori_loop(0, BLOCKS, mix, 0)

    def rs_first(b, way):
        return remote(
            ps.at[2, half_rows(b, way)], relay_in.at[way, b],
            rs_s.at[way, 0, b], rs_r.at[way, 0, b], beside[way],
        )

    def rs_plain(b, way):
        part = half_rows(b, 1 - way)
        return remote(
            ps.at[way, part], rin.at[way, part], rs_s.at[way, 1, b], rs_r.at[way, 1, b],
            beside[way],
        )

    def rs_added(b, way):
        part = half_rows(b, way)
        return remote(
            ps.at[way, part], rin.at[way, part], rs_s.at[way, 2, b], rs_r.at[way, 2, b],
            beside[way],
        )

    for way in range(2):
        ag_own(1, way).wait_recv()
        ag_relay(1, way).start()
    for slot, block in ((2, y_far), (0, y_next), (1, y_prev)):
        for b in range(BLOCKS):
            ps[slot, rows(b), :] = dot(normed[rows(b), :], w[:, columns(block)]).astype(BF16)
            if slot == 2:
                for way in range(2):
                    rs_first(b, way).start()
            else:
                rs_plain(b, slot).start()

    half = WIDTH // 2

    def core_out(j):
        return remote(wsend.at[j], wrecv.at[j], core_s.at[0, j], core_r.at[0, j], partner)

    def core_back(j):
        return remote(xg.at[j], pg.at[j], core_s.at[1, j], core_r.at[1, j], partner)

    def x_out(j, i):
        t = x_peer(i)
        return remote(
            xs.at[j, t], xb.at[j, x], wx_s.at[0, j, i], wx_r.at[0, j, i], at(z, t * 2 + c, y)
        )

    def x_back(j, i):
        t = x_peer(i)
        return remote(
            xg.at[j, x], xg.at[j, x], wx_s.at[1, j, i], wx_r.at[1, j, i], at(z, t * 2 + c, y)
        )

    def z_out(j, i):
        t = z_peer(i)
        return remote(
            zsw.at[j, t], zbw.at[j, z], wz_s.at[0, j, i], wz_r.at[0, j, i], at(t, r, y)
        )

    def z_back(j, i):
        t = z_peer(i)
        return remote(zone.at[j], zg.at[j, z], wz_s.at[1, j, i], wz_r.at[1, j, i], at(t, r, y))

    def w_start(j):
        theirs = pl.ds(pl.multiple_of(other * half, half), half)
        wsend[j] = dot(turned[theirs, :], gp[j]).astype(BF16)
        core_out(j).start()
        mine = pl.ds(pl.multiple_of(c * half, half), half)
        wown[j] = dot(turned[mine, :], gp[j])

    def w_x(j):
        core_out(j).wait_recv()
        for t in range(N_X):
            part = pl.ds(t * 64, 64)
            xs[j, t] = (wown[j, part, :] + wrecv[j, part, :].astype(F32)).astype(BF16)
        xb[j, x] = xs[j, x]
        loop(N_X, lambda i: x_out(j, i).start())

    def w_z(j):
        loop(
            N_X,
            lambda i: remote(
                xs.at[j, 0], xb.at[j, x_from(i)], wx_s.at[0, j, i], wx_r.at[0, j, i], partner
            ).wait_recv(),
        )
        total = xb[j, 0].astype(F32)
        for t in range(1, N_X):
            total = total + xb[j, t].astype(F32)
        total = total.astype(BF16)
        for t in range(N_Z):
            zsw[j, t] = total[(t // 2) * 16 : (t // 2) * 16 + 16, (t % 2) * 256 : (t % 2) * 256 + 256]
        zbw[j, z] = zsw[j, z]
        loop(N_Z, lambda i: z_out(j, i).start())

    def w_turn(j):
        loop(
            N_Z,
            lambda i: remote(
                zsw.at[j, 0], zbw.at[j, z_from(i)], wz_s.at[0, j, i], wz_r.at[0, j, i], partner
            ).wait_recv(),
        )
        total = zbw[j, 0].astype(F32)
        for t in range(1, N_Z):
            total = total + zbw[j, t].astype(F32)
        total = (total * GRAD_SCALE).astype(BF16)
        zone[j] = total
        zg[j, z] = total
        loop(N_Z, lambda i: z_back(j, i).start())

    def w_x_back(j):
        loop(
            N_Z,
            lambda i: remote(
                zone.at[j], zg.at[j, z_from(i)], wz_s.at[1, j, i], wz_r.at[1, j, i], partner
            ).wait_recv(),
        )
        pieces = [
            jnp.concatenate([zg[j, 2 * t], zg[j, 2 * t + 1]], axis=1) for t in range(N_Z // 2)
        ]
        xg[j, x] = jnp.concatenate(pieces, axis=0)
        loop(N_X, lambda i: x_back(j, i).start())

    def w_store(j, own_half):
        source = xg.at[j] if own_half else pg.at[j]
        start = (c if own_half else other) * N_X
        return pltpu.make_async_copy(
            source,
            gw_hbm.at[pl.ds(start, N_X), :, columns(model_block[j])],
            store_sem.at[4 + 2 * j + (0 if own_half else 1)],
        )

    def w_core_back(j):
        loop(
            N_X,
            lambda i: remote(
                xg.at[j, 0], xg.at[j, x_from(i)], wx_s.at[1, j, i], wx_r.at[1, j, i], partner
            ).wait_recv(),
        )
        core_back(j).start()
        w_store(j, True).start()

    def w_end(j):
        core_back(j).wait_recv()
        w_store(j, False).start()

    def w_sent(j):
        core_out(j).wait_send()
        core_back(j).wait_send()
        loop(N_X, lambda i: x_out(j, i).wait_send())
        loop(N_X, lambda i: x_back(j, i).wait_send())
        loop(N_Z, lambda i: z_out(j, i).wait_send())
        loop(N_Z, lambda i: z_back(j, i).wait_send())

    w_start(0)
    for way in range(2):
        ag_own(2, way).wait_recv()
        ag_relay(2, way).start()
    w_start(1)
    w_x(0)
    w_start(2)
    w_x(1)
    grad_normed(1, None)
    w_z(0)
    w_x(2)
    grad_normed(2, None)
    w_z(1)
    for b in range(BLOCKS):
        own[rows(b), :] = dot(normed[rows(b), :], w[:, columns(y)])
    w_turn(0)
    w_z(2)

    for b in range(BLOCKS):
        for way in range(2):
            ag_relay(b, way).wait_recv()

    w_start(3)
    grad_normed(3, None)

    def back_mix(b, _):
        at_rows = pl.ds(pl.multiple_of(b * SPAN, SPAN), SPAN)
        for h in range(HEADS):
            grad = gn[at_rows, head(h)]
            value = mixed[at_rows, head(h)]
            inverse = inv[at_rows, head(h)]
            mean = jnp.sum(grad * value, axis=1, keepdims=True) * (1.0 / HD)
            held = (inverse * (grad - value * inverse * inverse * mean)).astype(BF16)
            gm[at_rows, head(h)] = held
            gkv[b, h] = dot(q[at_rows, head(h)], held, TN)
        return 0

    lax.fori_loop(0, BLOCKS, back_mix, 0)
    fill(b_sb, gkv)
    scan_start(1, b_sb, b_rb)
    w_x(3)
    w_turn(1)
    w_x_back(0)

    def add_relayed(b):
        for way in range(2):
            rs_first(b, way).wait_recv()
            part = half_rows(b, way)
            both = ps[way, part, :].astype(F32) + relay_in[way, b].astype(F32)
            ps[way, part, :] = both.astype(BF16)
            rs_added(b, way).start()

    add_relayed(0)
    scan_middle(1, b_rb, b_zs, b_zb)
    w_z(3)
    add_relayed(1)
    w_turn(2)
    w_x_back(1)
    add_relayed(2)

    def back_local(b, _):
        at_rows = pl.ds(pl.multiple_of(b * SPAN, SPAN), SPAN)
        for h in range(HEADS):
            grad = gm[at_rows, head(h)]
            gs = dot(grad, v[at_rows, head(h)], NT)
            gs = jnp.where(causal, gs, 0.0).astype(BF16)
            gq_b[at_rows, head(h)] = (
                dot(grad, state[b * HEADS + h], NT) + dot(gs, k[at_rows, head(h)])
            ).astype(BF16)
            gk_acc[at_rows, head(h)] = dot(gs, q[at_rows, head(h)], TN)
            gv_acc[at_rows, head(h)] = dot(cs[b * HEADS + h], grad, TN)
        return 0

    lax.fori_loop(0, BLOCKS, back_local, 0)
    stores = [
        pltpu.make_async_copy(a, b, store_sem.at[i])
        for i, (a, b) in enumerate(
            ((gq_b, gq_hbm), (gk_b, gk_hbm), (gv_b, gv_hbm), (out_b, out_hbm))
        )
    ]
    stores[0].start()
    scan_late(1, b_rb, b_zb, b_pb, b_fb, True)
    w_core_back(0)
    w_turn(3)
    w_x_back(2)
    w_core_back(1)
    scan_end(1, b_fb)

    def back_end(b, _):
        at_rows = pl.ds(pl.multiple_of(b * SPAN, SPAN), SPAN)
        for h in range(HEADS):
            run = jnp.concatenate([b_fb[2 * h], b_fb[2 * h + 1]], axis=0).astype(F32)
            for later in range(1, BLOCKS):
                run = run + jnp.where(later > b, gkv[later, h], 0.0)
            held = run.astype(BF16)
            gk_b[at_rows, head(h)] = (
                gk_acc[at_rows, head(h)] + dot(v[at_rows, head(h)], held, NT)
            ).astype(BF16)
            gv_b[at_rows, head(h)] = (
                gv_acc[at_rows, head(h)] + dot(k[at_rows, head(h)], held)
            ).astype(BF16)
        return 0

    lax.fori_loop(0, BLOCKS, back_end, 0)
    stores[1].start()
    stores[2].start()
    w_x_back(3)
    w_core_back(2)
    w_end(0)
    w_end(1)
    w_core_back(3)
    w_end(2)

    for b in range(BLOCKS):
        for way in range(2):
            rs_plain(b, way).wait_recv()
    for b in range(BLOCKS):
        for way in range(2):
            rs_added(b, way).wait_recv()

        def finish(i, _):
            at_rows = pl.ds(pl.multiple_of(b * SPAN + i * 32, 32), 32)
            total = own[at_rows, :] + rin[0, at_rows, :].astype(F32) + rin[1, at_rows, :].astype(F32)
            out_b[at_rows, :] = (total * scale[at_rows, :]).astype(BF16)
            return 0

        lax.fori_loop(0, SPAN // 32, finish, 0)
    stores[3].start()
    w_end(3)

    for b in range(BLOCKS):
        for way in range(2):
            ag_own(b, way).wait_send()
            ag_relay(b, way).wait_send()
            rs_first(b, way).wait_send()
            rs_plain(b, way).wait_send()
            rs_added(b, way).wait_send()
    scan_sent(0, f_sb, f_rb, f_zs, f_zb, f_pb, f_fb)
    scan_sent(1, b_sb, b_rb, b_zs, b_zb, b_pb, b_fb)
    for j in range(4):
        w_sent(j)
        w_store(j, True).wait()
        w_store(j, False).wait()
    for store in stores:
        store.wait()


def local(queries, attn_keys, attn_values, out_weight, grad_out, drop_seed):
    square = (ROWS, WIDTH)
    vmem = pltpu.VMEM
    scan_buffers = [
        vmem((8, 64, 128), BF16),
        vmem((8, 64, 128), BF16),
        vmem((64, 128), BF16),
        vmem((8, 64, 128), BF16),
        vmem((8, 64, 128), BF16),
        vmem((8, 64, 128), BF16),
    ]
    dma = pltpu.SemaphoreType.DMA
    scratch = [
        vmem(square, BF16), vmem(square, BF16), vmem(square, BF16), vmem(square, BF16),
        vmem((WIDTH, MODEL), BF16),
        vmem(square, F32),
        vmem((4,) + square, BF16),
        vmem((BLOCKS, HEADS, HD, HD), F32),
        vmem((BLOCKS * HEADS, SPAN, SPAN), BF16),
        vmem((BLOCKS * HEADS, HD, HD), BF16),
        vmem(square, F32),
        vmem(square, F32),
        vmem(square, BF16),
        vmem((WIDTH, ROWS), BF16),
        vmem((3,) + square, BF16),
        vmem(square, F32),
        vmem((2, BLOCKS, HALF, WIDTH), BF16),
        vmem((2,) + square, BF16),
        vmem(square, F32),
        vmem(square, BF16),
        vmem((BLOCKS, HEADS, HD, HD), F32),
        vmem(square, F32), vmem(square, F32),
        vmem(square, BF16), vmem(square, BF16), vmem(square, BF16), vmem(square, BF16),
        *scan_buffers, *scan_buffers,
        vmem((4, 256, 512), BF16),
        vmem((4, 256, 512), F32),
        vmem((4, 256, 512), BF16),
        vmem((4, 4, 64, 512), BF16),
        vmem((4, 4, 64, 512), BF16),
        vmem((4, 8, 16, 256), BF16),
        vmem((4, 8, 16, 256), BF16),
        vmem((4, 16, 256), BF16),
        vmem((4, 8, 16, 256), BF16),
        vmem((4, 4, 64, 512), BF16),
        vmem((4, 4, 64, 512), BF16),
        dma((5,)), dma((12,)),
        dma((2, 3)), dma((2, 3)), dma((2, 3)), dma((2, 3)),
        dma((2, 3, 3)), dma((2, 3, 3)),
        dma((2, 3, 8)), dma((2, 3, 8)),
        dma((2, 4)), dma((2, 4)),
        dma((2, 4, 4)), dma((2, 4, 4)),
        dma((2, 4, 8)), dma((2, 4, 8)),
    ]
    hbm = pl.BlockSpec(memory_space=pl.ANY)
    outs = pl.pallas_call(
        kernel,
        out_shape=[jax.ShapeDtypeStruct(square, BF16)] * 4
        + [jax.ShapeDtypeStruct((8, 64, MODEL), BF16)],
        in_specs=[pl.BlockSpec(memory_space=pltpu.SMEM)] + [hbm] * 5,
        out_specs=[hbm] * 5,
        scratch_shapes=scratch,
        compiler_params=pltpu.CompilerParams(
            collective_id=0, has_side_effects=True, vmem_limit_bytes=60 * 1024 * 1024
        ),
        cost_estimate=pl.CostEstimate(
            flops=7_000_000_000, bytes_accessed=11_000_000, transcendentals=3072
        ),
        name="layer",
    )(drop_seed, queries, attn_keys, attn_values, out_weight, grad_out)
    output, grad_q, grad_k, grad_v, grad_w = outs
    return output, grad_q, grad_k, grad_v, grad_w.reshape(WIDTH, MODEL)


def solution(mesh):
    tokens = P("seq", "head")
    weight = P("head", None)
    return jax.shard_map(
        local,
        mesh=mesh,
        in_specs=(tokens, tokens, tokens, weight, tokens, P()),
        out_specs=(tokens, tokens, tokens, tokens, weight),
        check_vma=False,
    )
```

```python
import functools
import math

import jax
import jax.numpy as jnp
import numpy as np
from jax import lax
from jax.experimental import pallas as pl
from jax.experimental.pallas import tpu as pltpu
from jax.sharding import PartitionSpec as P

HD = 128
SPAN = 256
ROWS = 768
WIDTH = 512
MODEL = 2048
BLOCKS = ROWS // SPAN
HEADS = WIDTH // HD
N_ROW = 8
N_Z = 8
N_X = 4
HALF = SPAN // 2
EPS = 1e-05
KEEP_SCALE = 1.0 / 0.9
MODULUS = 32749.0
INVERSE = float(np.float32((1.0 - 2.0**-22) / 32749.0))
GRAD_SCALE = 1.0 / math.sqrt(49152)
MESH = pl.DeviceIdType.MESH
F32 = jnp.float32
BF16 = jnp.bfloat16

NN = (((1,), (0,)), ((), ()))
NT = (((1,), (1,)), ((), ()))
TN = (((0,), (0,)), ((), ()))


ORDER = (
    "go", "mask0", "states", "meet", "f1", "send0", "mask1", "send1", "mask2", "send2", "rest",
    "f2", "scores", "f3", "weight", "gn0", "relay0", "relay1", "relay2", "f4", "mix",
    "part_far", "w0_0", "part_next", "part_prev", "w1_0",
    "own", "w2_0", "near", "w0_1", "w0_2", "gn1", "gn2", "w1_1", "w1_2",
    "far", "gn3", "back_mix", "b1", "w0_3", "w3_0", "w1_3", "w2_1", "w2_2", "b2", "add0", "add1", "add2", "w2_3", "w4_0", "back_local",
    "w3_1", "w3_2", "b3", "w3_3", "w5_0", "w4_1", "w4_2", "b4", "back_end", "w4_3", "w6_0", "w5_1", "w5_2",
    "w5_3", "w6_1", "w6_2", "fin0", "fin1", "fin2", "w6_3",
)


def dot(a, b, dims=NN):
    return lax.dot_general(a, b, dims, preferred_element_type=F32)


def wrap(value):
    quotient = jnp.floor(value * INVERSE)
    rest = value - quotient * MODULUS
    return jnp.where(rest >= MODULUS, rest - MODULUS, rest)


def keep_scales(positions, features, seed):
    mixing = wrap((positions * 181 + seed).astype(F32) + (features * 227).astype(F32))
    whole = mixing.astype(jnp.int32)
    square = whole * whole
    quotient = jnp.floor(square.astype(F32) * INVERSE).astype(jnp.int32)
    rest = square - quotient * 32749
    rest = jnp.where(rest >= 32749, rest - 32749, rest).astype(F32)
    offsets = (positions * 7).astype(F32) + (features * 13).astype(F32)
    hashed = wrap(rest * 173.0 + mixing * 59.0 + offsets)
    tens = jnp.floor((hashed + 0.5) * 0.1)
    return jnp.where(hashed - tens * 10.0 != 0.0, KEEP_SCALE, 0.0).astype(F32)


def rows(block):
    return pl.ds(block * SPAN, SPAN)


def half_rows(block, half):
    return pl.ds(block * SPAN + half * HALF, HALF)


def head(h):
    return pl.ds(h * HD, HD)


def kernel(
    seed_ref, q_hbm, k_hbm, v_hbm, w_hbm, go_hbm,
    out_b, gq_b, gk_b, gv_b, gw_out,
    q, k, v, go, w, scale, gp, kv, cs, state, mixed, inv, normed, turned,
    ps, own, relay_in, rin, gn, gm, gkv, gk_acc, gv_acc,
    f_sb, f_rb, f_zs, f_zb, f_pb, f_fb, b_sb, b_rb, b_zs, b_zb, b_pb, b_fb,
    wsend, wown, wrecv, xs, xb, zsw, zbw, zone, zg, xg, pg,
    load_sem, ag_s, ag_r, agr_s, agr_r, rs_s, rs_r,
    scan_s, scan_r, core_s, core_r, wx_s, wx_r, wz_s, wz_r,
):
    seq = lax.axis_index("seq")
    y = lax.axis_index("head")
    z = seq // N_ROW
    r = seq % N_ROW
    x = r // 2
    c = r % 2
    other = 1 - c

    def at(zz, rr, yy):
        return {"seq": zz * N_ROW + rr, "head": yy}

    y_next, y_prev, y_far = (y + 1) % 4, (y + 3) % 4, (y + 2) % 4
    beside = (at(z, r, y_next), at(z, r, y_prev))
    partner = at(z, x * 2 + other, y)

    def row_peer(i):
        return (r + i) % N_ROW

    def z_peer(i):
        return (z + i) % N_Z

    def x_peer(i):
        return (x + i) % N_X

    def remote(src, dst, send, recv, device):
        return pltpu.make_async_remote_copy(
            src_ref=src, dst_ref=dst, send_sem=send, recv_sem=recv,
            device_id=device, device_id_type=MESH,
        )

    sent = []

    def loop(count, act):
        def step(i, _):
            act(i)
            return 0

        lax.fori_loop(1, count, step, 0)

    def start(copy):
        copy.start()
        sent.append(copy.wait_send)

    def start_all(count, make):
        loop(count, lambda i: make(i).start())
        sent.append(lambda: loop(count, lambda i: make(i).wait_send()))

    def put(copy):
        copy.start()
        sent.append(copy.wait)

    def arrive(copy):
        copy.wait_recv()

    def arrive_all(count, make):
        loop(count, lambda i: make(i).wait_recv())

    loads = [
        pltpu.make_async_copy(a, b, load_sem.at[i])
        for i, (a, b) in enumerate(
            ((go_hbm, go), (k_hbm, k), (v_hbm, v), (q_hbm, q), (w_hbm, w))
        )
    ]
    for load in loads:
        load.start()

    barrier = pltpu.get_barrier_semaphore()
    for device in beside:
        pl.semaphore_signal(barrier, inc=1, device_id=device, device_id_type=MESH)

    def greet(i, _):
        pl.semaphore_signal(
            barrier, inc=1, device_id=at(z, row_peer(i), y), device_id_type=MESH
        )
        pl.semaphore_signal(
            barrier, inc=1, device_id=at(z_peer(i), r, y), device_id_type=MESH
        )
        return 0

    lax.fori_loop(1, N_ROW, greet, 0)

    def ag_own(b, way, late):
        part = half_rows(b, 1 - way if late else way)
        return remote(
            gp.at[0, part], gp.at[1 + way, part], ag_s.at[way, late, b], ag_r.at[way, late, b],
            beside[way],
        )

    def ag_relay(b, way):
        part = half_rows(b, way)
        return remote(
            gp.at[1 + way, part], gp.at[3, part], agr_s.at[way, b], agr_r.at[way, b],
            beside[way],
        )

    seed = seed_ref[0]
    first_row = seq * ROWS
    first_column = y * WIDTH
    features = first_column + lax.broadcasted_iota(jnp.int32, (1, WIDTH), 1)
    TILE = 16

    def mask(b):
        def step(i, _):
            start = pl.multiple_of(b * SPAN + i * TILE, TILE)
            positions = first_row + start + lax.broadcasted_iota(jnp.int32, (TILE, 1), 0)
            kept = keep_scales(positions, features, seed)
            at_rows = pl.ds(start, TILE)
            scale[at_rows, :] = kept
            gp[0, at_rows, :] = (go[at_rows, :].astype(F32) * kept).astype(BF16)
            return 0

        lax.fori_loop(0, SPAN // TILE, step, 0)

    def block_states(b, _):
        at_rows = pl.ds(pl.multiple_of(b * SPAN, SPAN), SPAN)
        for h in range(HEADS):
            kv[b, h] = dot(k[at_rows, head(h)], v[at_rows, head(h)], TN)
        return 0

    def fill(sb, parts):
        for h in range(HEADS):
            total = (parts[0, h] + parts[1, h] + parts[2, h]).astype(BF16)
            sb[2 * h] = total[: HD // 2]
            sb[2 * h + 1] = total[HD // 2 :]

    def scan_one(n, i, sb, rb):
        t = row_peer(i)
        return remote(sb.at[t], rb.at[r], scan_s.at[n, 0, i], scan_r.at[n, 0, i], at(z, t, y))

    def scan_two(n, i, zs, zb):
        t = z_peer(i)
        return remote(zs, zb.at[z], scan_s.at[n, 1, i], scan_r.at[n, 1, i], at(t, r, y))

    def scan_three(n, i, pb, fb):
        t = row_peer(i)
        return remote(pb.at[t], fb.at[r], scan_s.at[n, 2, i], scan_r.at[n, 2, i], at(z, t, y))

    def row_from(i):
        return (r + N_ROW - i) % N_ROW

    def z_from(i):
        return (z + N_Z - i) % N_Z

    def x_from(i):
        return (x + N_X - i) % N_X

    def scan_start(n, sb, rb):
        rb[r] = sb[r]
        start_all(N_ROW, lambda i: scan_one(n, i, sb, rb))

    def scan_middle(n, rb, zs, zb):
        arrive_all(N_ROW, lambda i: remote(
                rb.at[0], rb.at[row_from(i)], scan_s.at[n, 0, i], scan_r.at[n, 0, i], partner
            ))
        total = rb[0].astype(F32)
        for j in range(1, N_ROW):
            total = total + rb[j].astype(F32)
        total = total.astype(BF16)
        zs[...] = total
        zb[z] = total
        start_all(N_Z, lambda i: scan_two(n, i, zs, zb))

    def scan_late(n, rb, zb, pb, fb, reverse):
        arrive_all(N_Z, lambda i: remote(
                zb.at[0], zb.at[z_from(i)], scan_s.at[n, 1, i], scan_r.at[n, 1, i], partner
            ))
        run = jnp.zeros((HD // 2, HD), F32)
        for j in range(N_Z):
            wanted = (j > z) if reverse else (j < z)
            run = run + jnp.where(wanted, zb[j].astype(F32), 0.0)
        order = range(N_ROW - 1, -1, -1) if reverse else range(N_ROW)
        for j in order:
            pb[j] = run.astype(BF16)
            run = run + rb[j].astype(F32)
        fb[r] = pb[r]
        start_all(N_ROW, lambda i: scan_three(n, i, pb, fb))

    def scan_end(n, fb):
        arrive_all(N_ROW, lambda i: remote(
                fb.at[0], fb.at[row_from(i)], scan_s.at[n, 2, i], scan_r.at[n, 2, i], partner
            ))

    causal = lax.broadcasted_iota(jnp.int32, (SPAN, SPAN), 0) >= lax.broadcasted_iota(
        jnp.int32, (SPAN, SPAN), 1
    )

    def scores(b, _):
        at_rows = pl.ds(pl.multiple_of(b * SPAN, SPAN), SPAN)
        for h in range(HEADS):
            value = dot(q[at_rows, head(h)], k[at_rows, head(h)], NT)
            value = jnp.where(causal, value, 0.0).astype(BF16)
            cs[b * HEADS + h] = value
            mixed[at_rows, head(h)] = dot(value, v[at_rows, head(h)])
        return 0

    def columns(block):
        return pl.ds(pl.multiple_of(block * WIDTH, WIDTH), WIDTH)

    model_block = (y, y_prev, y_next, y_far)

    def grad_normed(slot):
        def go_on(b, _):
            at_rows = pl.ds(pl.multiple_of(b * SPAN, SPAN), SPAN)
            term = dot(gp[slot, at_rows, :], w[:, columns(model_block[slot])], NT)
            gn[at_rows, :] = term if slot == 0 else gn[at_rows, :] + term
            return 0

        lax.fori_loop(0, BLOCKS, go_on, 0)

    def mix(b, _):
        at_rows = pl.ds(pl.multiple_of(b * SPAN, SPAN), SPAN)
        for h in range(HEADS):
            run = jnp.concatenate([f_fb[2 * h], f_fb[2 * h + 1]], axis=0).astype(F32)
            for earlier in range(BLOCKS - 1):
                run = run + jnp.where(earlier < b, kv[earlier, h], 0.0)
            held = run.astype(BF16)
            state[b * HEADS + h] = held
            value = mixed[at_rows, head(h)] + dot(q[at_rows, head(h)], held)
            mixed[at_rows, head(h)] = value
            power = jnp.sum(value * value, axis=1, keepdims=True) * (1.0 / HD)
            inverse = lax.rsqrt(power + EPS)
            inv[at_rows, head(h)] = jnp.broadcast_to(inverse, (SPAN, HD))
            normed[at_rows, head(h)] = (value * inverse).astype(BF16)
        turned[:, at_rows] = normed[at_rows, :].T
        return 0

    def rs_first(b, way):
        return remote(
            ps.at[2, half_rows(b, way)], relay_in.at[way, b],
            rs_s.at[way, 0, b], rs_r.at[way, 0, b], beside[way],
        )

    def rs_plain(b, way):
        part = half_rows(b, 1 - way)
        return remote(
            ps.at[way, part], rin.at[way, part], rs_s.at[way, 1, b], rs_r.at[way, 1, b],
            beside[way],
        )

    def rs_added(b, way):
        part = half_rows(b, way)
        return remote(
            ps.at[way, part], rin.at[way, part], rs_s.at[way, 2, b], rs_r.at[way, 2, b],
            beside[way],
        )

    def partial(slot, block):
        for b in range(BLOCKS):
            ps[slot, rows(b), :] = dot(normed[rows(b), :], w[:, columns(block)]).astype(BF16)
            if slot == 2:
                for way in range(2):
                    start(rs_first(b, way))
            else:
                start(rs_plain(b, slot))

    half = WIDTH // 2

    def core_out(j):
        return remote(wsend.at[j], wrecv.at[j], core_s.at[0, j], core_r.at[0, j], partner)

    def core_back(j):
        return remote(xg.at[j], pg.at[j], core_s.at[1, j], core_r.at[1, j], partner)

    def x_out(j, i):
        t = x_peer(i)
        return remote(
            xs.at[j, t], xb.at[j, x], wx_s.at[0, j, i], wx_r.at[0, j, i], at(z, t * 2 + c, y)
        )

    def x_back(j, i):
        t = x_peer(i)
        return remote(
            xg.at[j, x], xg.at[j, x], wx_s.at[1, j, i], wx_r.at[1, j, i], at(z, t * 2 + c, y)
        )

    def z_out(j, i):
        t = z_peer(i)
        return remote(
            zsw.at[j, t], zbw.at[j, z], wz_s.at[0, j, i], wz_r.at[0, j, i], at(t, r, y)
        )

    def z_back(j, i):
        t = z_peer(i)
        return remote(zone.at[j], zg.at[j, z], wz_s.at[1, j, i], wz_r.at[1, j, i], at(t, r, y))

    def w_start(j):
        theirs = pl.ds(pl.multiple_of(other * half, half), half)
        wsend[j] = dot(turned[theirs, :], gp[j]).astype(BF16)
        start(core_out(j))
        mine = pl.ds(pl.multiple_of(c * half, half), half)
        wown[j] = dot(turned[mine, :], gp[j])

    def w_x(j):
        arrive(core_out(j))
        for t in range(N_X):
            part = pl.ds(t * 64, 64)
            xs[j, t] = (wown[j, part, :] + wrecv[j, part, :].astype(F32)).astype(BF16)
        xb[j, x] = xs[j, x]
        start_all(N_X, lambda i: x_out(j, i))

    def w_z(j):
        arrive_all(N_X, lambda i: remote(
                xs.at[j, 0], xb.at[j, x_from(i)], wx_s.at[0, j, i], wx_r.at[0, j, i], partner
            ))
        total = xb[j, 0].astype(F32)
        for t in range(1, N_X):
            total = total + xb[j, t].astype(F32)
        total = total.astype(BF16)
        for t in range(N_Z):
            zsw[j, t] = total[(t // 2) * 16 : (t // 2) * 16 + 16, (t % 2) * 256 : (t % 2) * 256 + 256]
        zbw[j, z] = zsw[j, z]
        start_all(N_Z, lambda i: z_out(j, i))

    def w_turn(j):
        arrive_all(N_Z, lambda i: remote(
                zsw.at[j, 0], zbw.at[j, z_from(i)], wz_s.at[0, j, i], wz_r.at[0, j, i], partner
            ))
        total = zbw[j, 0].astype(F32)
        for t in range(1, N_Z):
            total = total + zbw[j, t].astype(F32)
        total = (total * GRAD_SCALE).astype(BF16)
        zone[j] = total
        zg[j, z] = total
        start_all(N_Z, lambda i: z_back(j, i))

    def w_x_back(j):
        arrive_all(N_Z, lambda i: remote(
                zone.at[j], zg.at[j, z_from(i)], wz_s.at[1, j, i], wz_r.at[1, j, i], partner
            ))
        pieces = [
            jnp.concatenate([zg[j, 2 * t], zg[j, 2 * t + 1]], axis=1) for t in range(N_Z // 2)
        ]
        xg[j, x] = jnp.concatenate(pieces, axis=0)
        start_all(N_X, lambda i: x_back(j, i))

    def w_store(j, own_half):
        source = xg if own_half else pg
        first = (c if own_half else other) * N_X
        for t in range(N_X):
            gw_out[first + t, :, columns(model_block[j])] = source[j, t]

    def w_core_back(j):
        arrive_all(N_X, lambda i: remote(
                xg.at[j, 0], xg.at[j, x_from(i)], wx_s.at[1, j, i], wx_r.at[1, j, i], partner
            ))
        start(core_back(j))
        w_store(j, True)

    def w_end(j):
        arrive(core_back(j))
        w_store(j, False)

    def back_mix(b, _):
        at_rows = pl.ds(pl.multiple_of(b * SPAN, SPAN), SPAN)
        for h in range(HEADS):
            grad = gn[at_rows, head(h)]
            value = mixed[at_rows, head(h)]
            inverse = inv[at_rows, head(h)]
            mean = jnp.sum(grad * value, axis=1, keepdims=True) * (1.0 / HD)
            held = (inverse * (grad - value * inverse * inverse * mean)).astype(BF16)
            gm[at_rows, head(h)] = held
            gkv[b, h] = dot(q[at_rows, head(h)], held, TN)
        return 0

    def add_relayed(b):
        for way in range(2):
            arrive(rs_first(b, way))
            part = half_rows(b, way)
            both = ps[way, part, :].astype(F32) + relay_in[way, b].astype(F32)
            ps[way, part, :] = both.astype(BF16)
            start(rs_added(b, way))

    def back_local(b, _):
        at_rows = pl.ds(pl.multiple_of(b * SPAN, SPAN), SPAN)
        for h in range(HEADS):
            grad = gm[at_rows, head(h)]
            gs = dot(grad, v[at_rows, head(h)], NT)
            gs = jnp.where(causal, gs, 0.0).astype(BF16)
            gq_b[at_rows, head(h)] = (
                dot(grad, state[b * HEADS + h], NT) + dot(gs, k[at_rows, head(h)])
            ).astype(BF16)
            gk_acc[at_rows, head(h)] = dot(gs, q[at_rows, head(h)], TN)
            gv_acc[at_rows, head(h)] = dot(cs[b * HEADS + h], grad, TN)
        return 0

    def back_end(b, _):
        at_rows = pl.ds(pl.multiple_of(b * SPAN, SPAN), SPAN)
        for h in range(HEADS):
            run = jnp.concatenate([b_fb[2 * h], b_fb[2 * h + 1]], axis=0).astype(F32)
            for later in range(1, BLOCKS):
                run = run + jnp.where(later > b, gkv[later, h], 0.0)
            held = run.astype(BF16)
            gk_b[at_rows, head(h)] = (
                gk_acc[at_rows, head(h)] + dot(v[at_rows, head(h)], held, NT)
            ).astype(BF16)
            gv_b[at_rows, head(h)] = (
                gv_acc[at_rows, head(h)] + dot(k[at_rows, head(h)], held)
            ).astype(BF16)
        return 0

    def finish(b):
        for way in range(2):
            arrive(rs_plain(b, way))
            arrive(rs_added(b, way))

        def step(i, _):
            at_rows = pl.ds(pl.multiple_of(b * SPAN + i * 32, 32), 32)
            total = own[at_rows, :] + rin[0, at_rows, :].astype(F32) + rin[1, at_rows, :].astype(F32)
            out_b[at_rows, :] = (total * scale[at_rows, :]).astype(BF16)
            return 0

        lax.fori_loop(0, SPAN // 32, step, 0)

    def blocks(body):
        lax.fori_loop(0, BLOCKS, body, 0)

    def do_send(b):
        for way in range(2):
            start(ag_own(b, way, 0))

    def do_rest():
        for b in range(BLOCKS):
            for way in range(2):
                start(ag_own(b, way, 1))

    def do_relay(b):
        for way in range(2):
            arrive(ag_own(b, way, 0))
            start(ag_relay(b, way))

    def do_near():
        for b in range(BLOCKS):
            for way in range(2):
                arrive(ag_own(b, way, 1))

    def do_far():
        for b in range(BLOCKS):
            for way in range(2):
                arrive(ag_relay(b, way))

    def do_states():
        loads[1].wait()
        loads[2].wait()
        blocks(block_states)
        fill(f_sb, kv)

    def do_scores():
        loads[3].wait()
        blocks(scores)

    def do_own():
        for b in range(BLOCKS):
            own[rows(b), :] = dot(normed[rows(b), :], w[:, columns(y)])

    def do_back_mix():
        blocks(back_mix)
        fill(b_sb, gkv)

    def do_back_local():
        blocks(back_local)

    def do_back_end():
        blocks(back_end)

    steps = {
        "go": loads[0].wait,
        "weight": loads[4].wait,
        "meet": lambda: pl.semaphore_wait(barrier, 2 + N_ROW - 1 + N_Z - 1),
        "states": do_states,
        "scores": do_scores,
        "mix": lambda: blocks(mix),
        "rest": do_rest,
        "near": do_near,
        "far": do_far,
        "back_mix": do_back_mix,
        "back_local": do_back_local,
        "back_end": do_back_end,
        "own": do_own,
        "part_far": lambda: partial(2, y_far),
        "part_next": lambda: partial(0, y_next),
        "part_prev": lambda: partial(1, y_prev),
        "f1": lambda: scan_start(0, f_sb, f_rb),
        "f2": lambda: scan_middle(0, f_rb, f_zs, f_zb),
        "f3": lambda: scan_late(0, f_rb, f_zb, f_pb, f_fb, False),
        "f4": lambda: scan_end(0, f_fb),
        "b1": lambda: scan_start(1, b_sb, b_rb),
        "b2": lambda: scan_middle(1, b_rb, b_zs, b_zb),
        "b3": lambda: scan_late(1, b_rb, b_zb, b_pb, b_fb, True),
        "b4": lambda: scan_end(1, b_fb),
    }
    for b in range(BLOCKS):
        steps[f"mask{b}"] = functools.partial(mask, b)
        steps[f"send{b}"] = functools.partial(do_send, b)
        steps[f"relay{b}"] = functools.partial(do_relay, b)
        steps[f"add{b}"] = functools.partial(add_relayed, b)
        steps[f"fin{b}"] = functools.partial(finish, b)
    for j in range(4):
        steps[f"gn{j}"] = functools.partial(grad_normed, j)
        for n, act in enumerate((w_start, w_x, w_z, w_turn, w_x_back, w_core_back, w_end)):
            steps[f"w{n}_{j}"] = functools.partial(act, j)
    for name in ORDER:
        steps[name]()

    for wait in sent:
        wait()


def write_out(*refs):
    sources, targets, done = refs[:5], refs[5:10], refs[10]
    copies = [
        pltpu.make_async_copy(a, b, done.at[i]) for i, (a, b) in enumerate(zip(sources, targets))
    ]
    for copy in copies:
        copy.start()
    for copy in copies:
        copy.wait()


def local(queries, attn_keys, attn_values, out_weight, grad_out, drop_seed):
    square = (ROWS, WIDTH)
    vmem = pltpu.VMEM
    scan_buffers = [
        vmem((8, 64, 128), BF16),
        vmem((8, 64, 128), BF16),
        vmem((64, 128), BF16),
        vmem((8, 64, 128), BF16),
        vmem((8, 64, 128), BF16),
        vmem((8, 64, 128), BF16),
    ]
    dma = pltpu.SemaphoreType.DMA
    scratch = [
        vmem(square, BF16), vmem(square, BF16), vmem(square, BF16), vmem(square, BF16),
        vmem((WIDTH, MODEL), BF16),
        vmem(square, F32),
        vmem((4,) + square, BF16),
        vmem((BLOCKS, HEADS, HD, HD), F32),
        vmem((BLOCKS * HEADS, SPAN, SPAN), BF16),
        vmem((BLOCKS * HEADS, HD, HD), BF16),
        vmem(square, F32),
        vmem(square, F32),
        vmem(square, BF16),
        vmem((WIDTH, ROWS), BF16),
        vmem((3,) + square, BF16),
        vmem(square, F32),
        vmem((2, BLOCKS, HALF, WIDTH), BF16),
        vmem((2,) + square, BF16),
        vmem(square, F32),
        vmem(square, BF16),
        vmem((BLOCKS, HEADS, HD, HD), F32),
        vmem(square, F32), vmem(square, F32),
        *scan_buffers, *scan_buffers,
        vmem((4, 256, 512), BF16),
        vmem((4, 256, 512), F32),
        vmem((4, 256, 512), BF16),
        vmem((4, 4, 64, 512), BF16),
        vmem((4, 4, 64, 512), BF16),
        vmem((4, 8, 16, 256), BF16),
        vmem((4, 8, 16, 256), BF16),
        vmem((4, 16, 256), BF16),
        vmem((4, 8, 16, 256), BF16),
        vmem((4, 4, 64, 512), BF16),
        vmem((4, 4, 64, 512), BF16),
        dma((5,)),
        dma((2, 2, 3)), dma((2, 2, 3)), dma((2, 3)), dma((2, 3)),
        dma((2, 3, 3)), dma((2, 3, 3)),
        dma((2, 3, 8)), dma((2, 3, 8)),
        dma((2, 4)), dma((2, 4)),
        dma((2, 4, 4)), dma((2, 4, 4)),
        dma((2, 4, 8)), dma((2, 4, 8)),
    ]
    hbm = pl.BlockSpec(memory_space=pl.ANY)
    outs = pl.pallas_call(
        kernel,
        out_shape=[vmem(square, BF16)] * 4 + [vmem((8, 64, MODEL), BF16)],
        in_specs=[pl.BlockSpec(memory_space=pltpu.SMEM)] + [hbm] * 5,
        out_specs=[pl.BlockSpec(memory_space=vmem)] * 5,
        scratch_shapes=scratch,
        compiler_params=pltpu.CompilerParams(
            collective_id=0, has_side_effects=True, vmem_limit_bytes=56 * 1024 * 1024
        ),
        cost_estimate=pl.CostEstimate(
            flops=7_000_000_000, bytes_accessed=11_000_000, transcendentals=3072
        ),
        name="layer",
    )(drop_seed, queries, attn_keys, attn_values, out_weight, grad_out)
    output, grad_q, grad_k, grad_v, grad_w = pl.pallas_call(
        write_out,
        out_shape=[jax.ShapeDtypeStruct(square, BF16)] * 4
        + [jax.ShapeDtypeStruct((8, 64, MODEL), BF16)],
        in_specs=[pl.BlockSpec(memory_space=vmem)] * 5,
        out_specs=[hbm] * 5,
        scratch_shapes=[dma((5,))],
        name="write_out",
    )(*outs)
    return output, grad_q, grad_k, grad_v, grad_w.reshape(WIDTH, MODEL)


def solution(mesh):
    tokens = P("seq", "head")
    weight = P("head", None)
    return jax.shard_map(
        local,
        mesh=mesh,
        in_specs=(tokens, tokens, tokens, weight, tokens, P()),
        out_specs=(tokens, tokens, tokens, tokens, weight),
        check_vma=False,
    )
```

```python
import functools
import math

import jax
import jax.numpy as jnp
import numpy as np
from jax import lax
from jax.experimental import pallas as pl
from jax.experimental.pallas import tpu as pltpu
from jax.sharding import PartitionSpec as P

HD = 128
SPAN = 256
ROWS = 768
WIDTH = 512
MODEL = 2048
BLOCKS = ROWS // SPAN
HEADS = WIDTH // HD
N_ROW = 8
N_Z = 8
N_X = 4
HALF = SPAN // 2
EPS = 1e-05
KEEP_SCALE = 1.0 / 0.9
MODULUS = 32749.0
INVERSE = float(np.float32((1.0 - 2.0**-22) / 32749.0))
GRAD_SCALE = 1.0 / math.sqrt(49152)
MESH = pl.DeviceIdType.MESH
F32 = jnp.float32
BF16 = jnp.bfloat16

NN = (((1,), (0,)), ((), ()))
NT = (((1,), (1,)), ((), ()))
TN = (((0,), (0,)), ((), ()))


ORDER = (
    "go", "mask0", "states", "meet", "f1", "send0", "mask1", "send1", "mask2", "send2", "rest",
    "f2", "scores", "f3", "weight", "gn0", "f4", "relay0", "relay1", "relay2", "mix",
    "w0_0", "part_far", "part_next", "part_prev", "w1_0", "near", "w0_1", "w0_2", "gn1", "gn2", "own", "w1_1", "w1_2", "w2_0",
    "far0", "far1", "far2", "w0_3", "fill", "b1", "w1_3", "w2_1", "w2_2", "w3_0", "add0", "add1", "add2", "b2", "local0", "w2_3", "w4_0", "w3_1", "w3_2",
    "local1", "b3", "local2", "w3_3", "w4_1", "w4_2", "w5_0", "b4", "back_end", "w4_3", "w5_1", "w5_2", "w6_0", "w6_1", "w6_2", "fin0", "w5_3", "fin1", "fin2", "w6_3",
)


def dot(a, b, dims=NN):
    return lax.dot_general(a, b, dims, preferred_element_type=F32)


def wrap(value):
    quotient = jnp.floor(value * INVERSE)
    rest = value - quotient * MODULUS
    return jnp.where(rest >= MODULUS, rest - MODULUS, rest)


def keep_scales(positions, features, seed):
    mixing = wrap((positions * 181 + seed).astype(F32) + (features * 227).astype(F32))
    whole = mixing.astype(jnp.int32)
    square = whole * whole
    quotient = jnp.floor(square.astype(F32) * INVERSE).astype(jnp.int32)
    rest = square - quotient * 32749
    rest = jnp.where(rest >= 32749, rest - 32749, rest).astype(F32)
    offsets = (positions * 7).astype(F32) + (features * 13).astype(F32)
    hashed = wrap(rest * 173.0 + mixing * 59.0 + offsets)
    tens = jnp.floor((hashed + 0.5) * 0.1)
    return jnp.where(hashed - tens * 10.0 != 0.0, KEEP_SCALE, 0.0).astype(F32)


def rows(block):
    return pl.ds(block * SPAN, SPAN)


def half_rows(block, half):
    return pl.ds(block * SPAN + half * HALF, HALF)


def head(h):
    return pl.ds(h * HD, HD)


def kernel(
    seed_hbm, q_hbm, k_hbm, v_hbm, w_hbm, go_hbm,
    out_b, gq_b, gk_b, gv_b, gw_out,
    q, k, v, go, w, scale, gp, kv, cs, state, mixed, inv, normed, turned,
    ps, own, relay_in, rin, gn, gm, gkv, gk_acc, gv_acc,
    f_sb, f_rb, f_zs, f_zb, f_pb, f_fb, b_sb, b_rb, b_zs, b_zb, b_pb, b_fb,
    seed_ref, wsend, wown, wrecv, xs, xb, zsw, zbw, zone, zg, xg, pg,
    load_sem, ag_s, ag_r, rs_s, rs_r, scan_s, scan_r, w_s, w_r,
):
    seq = lax.axis_index("seq")
    y = lax.axis_index("head")
    z = seq // N_ROW
    r = seq % N_ROW
    x = r // 2
    c = r % 2
    other = 1 - c

    def at(zz, rr, yy):
        return {"seq": zz * N_ROW + rr, "head": yy}

    y_next, y_prev, y_far = (y + 1) % 4, (y + 3) % 4, (y + 2) % 4
    beside = (at(z, r, y_next), at(z, r, y_prev))
    partner = at(z, x * 2 + other, y)

    def row_peer(i):
        return (r + i) % N_ROW

    def z_peer(i):
        return (z + i) % N_Z

    def x_peer(i):
        return (x + i) % N_X

    def remote(src, dst, send, recv, device):
        return pltpu.make_async_remote_copy(
            src_ref=src, dst_ref=dst, send_sem=send, recv_sem=recv,
            device_id=device, device_id_type=MESH,
        )

    def loop(count, act):
        def step(i, _):
            act(i)
            return 0

        lax.fori_loop(1, count, step, 0)

    def start(copy):
        copy.start()

    def start_all(count, make):
        loop(count, lambda i: make(i).start())

    def arrive(ref, sem):
        remote(ref, ref, sem, sem, partner).wait_recv()

    def left(ref, sem):
        remote(ref, ref, sem, sem, partner).wait_send()

    barrier = pltpu.get_barrier_semaphore()
    for device in beside:
        pl.semaphore_signal(barrier, inc=1, device_id=device, device_id_type=MESH)

    def greet(i, _):
        pl.semaphore_signal(
            barrier, inc=1, device_id=at(z, row_peer(i), y), device_id_type=MESH
        )
        pl.semaphore_signal(
            barrier, inc=1, device_id=at(z_peer(i), r, y), device_id_type=MESH
        )
        return 0

    lax.fori_loop(1, N_ROW, greet, 0)

    loads = [
        pltpu.make_async_copy(a, b, load_sem.at[i])
        for i, (a, b) in enumerate(
            (
                (go_hbm, go), (k_hbm, k), (v_hbm, v), (q_hbm, q), (w_hbm, w),
                (seed_hbm, seed_ref),
            )
        )
    ]
    loads[5].start()
    for load in loads[:5]:
        load.start()

    def ag_own(b, way, late):
        part = half_rows(b, 1 - way if late else way)
        return remote(
            gp.at[0, part], gp.at[1 + way, part], ag_s.at[0], ag_r.at[3 if late else b],
            beside[way],
        )

    def ag_relay(b, way):
        part = half_rows(b, way)
        return remote(
            gp.at[1 + way, part], gp.at[3, part], ag_s.at[1], ag_r.at[4 + b],
            beside[way],
        )

    first_row = seq * ROWS
    first_column = y * WIDTH
    features = first_column + lax.broadcasted_iota(jnp.int32, (1, WIDTH), 1)
    TILE = 16

    def mask(b):
        seed = seed_ref[0]

        def step(i, _):
            start = pl.multiple_of(b * SPAN + i * TILE, TILE)
            positions = first_row + start + lax.broadcasted_iota(jnp.int32, (TILE, 1), 0)
            kept = keep_scales(positions, features, seed)
            at_rows = pl.ds(start, TILE)
            scale[at_rows, :] = kept
            gp[0, at_rows, :] = (go[at_rows, :].astype(F32) * kept).astype(BF16)
            return 0

        lax.fori_loop(0, SPAN // TILE, step, 0)

    def block_states(b, _):
        at_rows = pl.ds(pl.multiple_of(b * SPAN, SPAN), SPAN)
        for h in range(HEADS):
            kv[b, h] = dot(k[at_rows, head(h)], v[at_rows, head(h)], TN)
        return 0

    def fill(sb, parts):
        for h in range(HEADS):
            total = (parts[0, h] + parts[1, h] + parts[2, h]).astype(BF16)
            sb[2 * h] = total[: HD // 2]
            sb[2 * h + 1] = total[HD // 2 :]

    def scan_one(n, i, sb, rb):
        t = row_peer(i)
        return remote(sb.at[t], rb.at[r], scan_s.at[n, 0], scan_r.at[n, 0], at(z, t, y))

    def scan_two(n, i, zs, zb):
        t = z_peer(i)
        return remote(zs, zb.at[z], scan_s.at[n, 1], scan_r.at[n, 1], at(t, r, y))

    def scan_three(n, i, pb, fb):
        t = row_peer(i)
        return remote(pb.at[t], fb.at[r], scan_s.at[n, 2], scan_r.at[n, 2], at(z, t, y))

    def scan_start(n, sb, rb):
        rb[r] = sb[r]
        start_all(N_ROW, lambda i: scan_one(n, i, sb, rb))

    def scan_middle(n, rb, zs, zb):
        arrive(rb.at[pl.ds(0, N_ROW - 1)], scan_r.at[n, 0])
        total = rb[0].astype(F32)
        for j in range(1, N_ROW):
            total = total + rb[j].astype(F32)
        total = total.astype(BF16)
        zs[...] = total
        zb[z] = total
        start_all(N_Z, lambda i: scan_two(n, i, zs, zb))

    def scan_late(n, rb, zb, pb, fb, reverse):
        arrive(zb.at[pl.ds(0, N_Z - 1)], scan_r.at[n, 1])
        run = jnp.zeros((HD // 2, HD), F32)
        for j in range(N_Z):
            wanted = (j > z) if reverse else (j < z)
            run = run + jnp.where(wanted, zb[j].astype(F32), 0.0)
        order = range(N_ROW - 1, -1, -1) if reverse else range(N_ROW)
        for j in order:
            pb[j] = run.astype(BF16)
            run = run + rb[j].astype(F32)
        fb[r] = pb[r]
        start_all(N_ROW, lambda i: scan_three(n, i, pb, fb))

    def scan_end(n, fb):
        arrive(fb.at[pl.ds(0, N_ROW - 1)], scan_r.at[n, 2])

    causal = lax.broadcasted_iota(jnp.int32, (SPAN, SPAN), 0) >= lax.broadcasted_iota(
        jnp.int32, (SPAN, SPAN), 1
    )

    def scores(b, _):
        at_rows = pl.ds(pl.multiple_of(b * SPAN, SPAN), SPAN)
        for h in range(HEADS):
            value = dot(q[at_rows, head(h)], k[at_rows, head(h)], NT)
            value = jnp.where(causal, value, 0.0).astype(BF16)
            cs[b * HEADS + h] = value
            mixed[at_rows, head(h)] = dot(value, v[at_rows, head(h)])
        return 0

    def columns(block):
        return pl.ds(pl.multiple_of(block * WIDTH, WIDTH), WIDTH)

    model_block = (y, y_prev, y_next, y_far)

    def add_grad_normed(slot, b):
        at_rows = pl.ds(pl.multiple_of(b * SPAN, SPAN), SPAN)
        term = dot(gp[slot, at_rows, :], w[:, columns(model_block[slot])], NT)
        gn[at_rows, :] = term if slot == 0 else gn[at_rows, :] + term

    def grad_normed(slot):
        def go_on(b, _):
            add_grad_normed(slot, b)
            return 0

        lax.fori_loop(0, BLOCKS, go_on, 0)

    def mix(b, _):
        at_rows = pl.ds(pl.multiple_of(b * SPAN, SPAN), SPAN)
        for h in range(HEADS):
            run = jnp.concatenate([f_fb[2 * h], f_fb[2 * h + 1]], axis=0).astype(F32)
            for earlier in range(BLOCKS - 1):
                run = run + jnp.where(earlier < b, kv[earlier, h], 0.0)
            held = run.astype(BF16)
            state[b * HEADS + h] = held
            value = mixed[at_rows, head(h)] + dot(q[at_rows, head(h)], held)
            mixed[at_rows, head(h)] = value
            power = jnp.sum(value * value, axis=1, keepdims=True) * (1.0 / HD)
            inverse = lax.rsqrt(power + EPS)
            inv[at_rows, head(h)] = jnp.broadcast_to(inverse, (SPAN, HD))
            normed[at_rows, head(h)] = (value * inverse).astype(BF16)
        turned[:, at_rows] = normed[at_rows, :].T
        return 0

    def rs_first(b, way):
        return remote(
            ps.at[2, half_rows(b, way)], relay_in.at[way, b],
            rs_s.at[0], rs_r.at[b], beside[way],
        )

    def rs_plain(b, way):
        part = half_rows(b, 1 - way)
        return remote(
            ps.at[way, part], rin.at[way, part], rs_s.at[1], rs_r.at[3 + b],
            beside[way],
        )

    def rs_added(b, way):
        part = half_rows(b, way)
        return remote(
            ps.at[way, part], rin.at[way, part], rs_s.at[1], rs_r.at[3 + b],
            beside[way],
        )

    def partial(slot, block):
        for b in range(BLOCKS):
            ps[slot, rows(b), :] = dot(normed[rows(b), :], w[:, columns(block)]).astype(BF16)
            if slot == 2:
                for way in range(2):
                    start(rs_first(b, way))
            else:
                start(rs_plain(b, slot))

    half = WIDTH // 2

    def core_out(j):
        return remote(wsend.at[j], wrecv.at[j], w_s.at[0], w_r.at[0, j], partner)

    def core_back(j):
        return remote(xg.at[j], pg.at[j], w_s.at[1], w_r.at[1, j], partner)

    def x_out(j, i):
        t = x_peer(i)
        return remote(
            xs.at[j, t], xb.at[j, x], w_s.at[2], w_r.at[2, j], at(z, t * 2 + c, y)
        )

    def x_back(j, i):
        t = x_peer(i)
        return remote(
            xg.at[j, x], xg.at[j, x], w_s.at[3], w_r.at[3, j], at(z, t * 2 + c, y)
        )

    def z_out(j, i):
        t = z_peer(i)
        return remote(
            zsw.at[j, t], zbw.at[j, z], w_s.at[4], w_r.at[4, j], at(t, r, y)
        )

    def z_back(j, i):
        t = z_peer(i)
        return remote(zone.at[j], zg.at[j, z], w_s.at[5], w_r.at[5, j], at(t, r, y))

    def w_start(j):
        theirs = pl.ds(pl.multiple_of(other * half, half), half)
        wsend[j] = dot(turned[theirs, :], gp[j]).astype(BF16)
        start(core_out(j))
        mine = pl.ds(pl.multiple_of(c * half, half), half)
        wown[j] = dot(turned[mine, :], gp[j])

    def w_x(j):
        arrive(wrecv.at[j], w_r.at[0, j])
        for t in range(N_X):
            part = pl.ds(t * 64, 64)
            xs[j, t] = (wown[j, part, :] + wrecv[j, part, :].astype(F32)).astype(BF16)
        xb[j, x] = xs[j, x]
        start_all(N_X, lambda i: x_out(j, i))

    def w_z(j):
        arrive(xb.at[j, pl.ds(0, N_X - 1)], w_r.at[2, j])
        total = xb[j, 0].astype(F32)
        for t in range(1, N_X):
            total = total + xb[j, t].astype(F32)
        total = total.astype(BF16)
        for t in range(N_Z):
            zsw[j, t] = total[(t // 2) * 16 : (t // 2) * 16 + 16, (t % 2) * 256 : (t % 2) * 256 + 256]
        zbw[j, z] = zsw[j, z]
        start_all(N_Z, lambda i: z_out(j, i))

    def w_turn(j):
        arrive(zbw.at[j, pl.ds(0, N_Z - 1)], w_r.at[4, j])
        total = zbw[j, 0].astype(F32)
        for t in range(1, N_Z):
            total = total + zbw[j, t].astype(F32)
        total = (total * GRAD_SCALE).astype(BF16)
        zone[j] = total
        zg[j, z] = total
        start_all(N_Z, lambda i: z_back(j, i))

    def w_x_back(j):
        arrive(zg.at[j, pl.ds(0, N_Z - 1)], w_r.at[5, j])
        pieces = [
            jnp.concatenate([zg[j, 2 * t], zg[j, 2 * t + 1]], axis=1) for t in range(N_Z // 2)
        ]
        xg[j, x] = jnp.concatenate(pieces, axis=0)
        start_all(N_X, lambda i: x_back(j, i))

    def w_store(j, own_half):
        source = xg if own_half else pg
        first = (c if own_half else other) * N_X
        for t in range(N_X):
            gw_out[first + t, :, columns(model_block[j])] = source[j, t]

    def w_core_back(j):
        arrive(xg.at[j, pl.ds(0, N_X - 1)], w_r.at[3, j])
        start(core_back(j))
        w_store(j, True)

    def w_end(j):
        arrive(pg.at[j], w_r.at[1, j])
        w_store(j, False)

    def back_mix(b, _):
        at_rows = pl.ds(pl.multiple_of(b * SPAN, SPAN), SPAN)
        for h in range(HEADS):
            grad = gn[at_rows, head(h)]
            value = mixed[at_rows, head(h)]
            inverse = inv[at_rows, head(h)]
            mean = jnp.sum(grad * value, axis=1, keepdims=True) * (1.0 / HD)
            held = (inverse * (grad - value * inverse * inverse * mean)).astype(BF16)
            gm[at_rows, head(h)] = held
            gkv[b, h] = dot(q[at_rows, head(h)], held, TN)
        return 0

    def add_relayed(b):
        arrive(relay_in.at[:, b], rs_r.at[b])
        for way in range(2):
            part = half_rows(b, way)
            both = ps[way, part, :].astype(F32) + relay_in[way, b].astype(F32)
            ps[way, part, :] = both.astype(BF16)
            start(rs_added(b, way))

    def back_local(b, _):
        at_rows = pl.ds(pl.multiple_of(b * SPAN, SPAN), SPAN)
        for h in range(HEADS):
            grad = gm[at_rows, head(h)]
            gs = dot(grad, v[at_rows, head(h)], NT)
            gs = jnp.where(causal, gs, 0.0).astype(BF16)
            gq_b[at_rows, head(h)] = (
                dot(grad, state[b * HEADS + h], NT) + dot(gs, k[at_rows, head(h)])
            ).astype(BF16)
            gk_acc[at_rows, head(h)] = dot(gs, q[at_rows, head(h)], TN)
            gv_acc[at_rows, head(h)] = dot(cs[b * HEADS + h], grad, TN)
        return 0

    def back_end(b, _):
        at_rows = pl.ds(pl.multiple_of(b * SPAN, SPAN), SPAN)
        for h in range(HEADS):
            run = jnp.concatenate([b_fb[2 * h], b_fb[2 * h + 1]], axis=0).astype(F32)
            for later in range(1, BLOCKS):
                run = run + jnp.where(later > b, gkv[later, h], 0.0)
            held = run.astype(BF16)
            gk_b[at_rows, head(h)] = (
                gk_acc[at_rows, head(h)] + dot(v[at_rows, head(h)], held, NT)
            ).astype(BF16)
            gv_b[at_rows, head(h)] = (
                gv_acc[at_rows, head(h)] + dot(k[at_rows, head(h)], held)
            ).astype(BF16)
        return 0

    def finish(b):
        arrive(rin.at[:, rows(b)], rs_r.at[3 + b])

        def step(i, _):
            at_rows = pl.ds(pl.multiple_of(b * SPAN + i * 32, 32), 32)
            total = own[at_rows, :] + rin[0, at_rows, :].astype(F32) + rin[1, at_rows, :].astype(F32)
            out_b[at_rows, :] = (total * scale[at_rows, :]).astype(BF16)
            return 0

        lax.fori_loop(0, SPAN // 32, step, 0)

    def blocks(body):
        lax.fori_loop(0, BLOCKS, body, 0)

    def do_send(b):
        for way in range(2):
            start(ag_own(b, way, 0))

    def do_rest():
        for b in range(BLOCKS):
            for way in range(2):
                start(ag_own(b, way, 1))

    def do_relay(b):
        arrive(gp.at[1, rows(b)], ag_r.at[b])
        for way in range(2):
            start(ag_relay(b, way))

    def do_near():
        arrive(gp.at[1], ag_r.at[3])

    def do_far(b):
        arrive(gp.at[3, rows(b)], ag_r.at[4 + b])

    def do_states():
        loads[1].wait()
        loads[2].wait()
        blocks(block_states)
        fill(f_sb, kv)

    def do_scores():
        loads[3].wait()
        blocks(scores)

    def do_own():
        for b in range(BLOCKS):
            own[rows(b), :] = dot(normed[rows(b), :], w[:, columns(y)])

    def do_far_mix(b):
        do_far(b)
        add_grad_normed(3, b)
        back_mix(b, 0)

    def do_back_end():
        blocks(back_end)

    steps = {
        "go": lambda: (loads[5].wait(), loads[0].wait()),
        "weight": loads[4].wait,
        "meet": lambda: pl.semaphore_wait(barrier, 2 + N_ROW - 1 + N_Z - 1),
        "states": do_states,
        "scores": do_scores,
        "mix": lambda: blocks(mix),
        "rest": do_rest,
        "near": do_near,
        "fill": lambda: fill(b_sb, gkv),
        "back_end": do_back_end,
        "own": do_own,
        "part_far": lambda: partial(2, y_far),
        "part_next": lambda: partial(0, y_next),
        "part_prev": lambda: partial(1, y_prev),
        "f1": lambda: scan_start(0, f_sb, f_rb),
        "f2": lambda: scan_middle(0, f_rb, f_zs, f_zb),
        "f3": lambda: scan_late(0, f_rb, f_zb, f_pb, f_fb, False),
        "f4": lambda: scan_end(0, f_fb),
        "b1": lambda: scan_start(1, b_sb, b_rb),
        "b2": lambda: scan_middle(1, b_rb, b_zs, b_zb),
        "b3": lambda: scan_late(1, b_rb, b_zb, b_pb, b_fb, True),
        "b4": lambda: scan_end(1, b_fb),
    }
    for b in range(BLOCKS):
        steps[f"mask{b}"] = functools.partial(mask, b)
        steps[f"send{b}"] = functools.partial(do_send, b)
        steps[f"relay{b}"] = functools.partial(do_relay, b)
        steps[f"add{b}"] = functools.partial(add_relayed, b)
        steps[f"local{b}"] = functools.partial(back_local, b, 0)
        steps[f"fin{b}"] = functools.partial(finish, b)
        steps[f"far{b}"] = functools.partial(do_far_mix, b)
    for j in range(4):
        steps[f"gn{j}"] = functools.partial(grad_normed, j)
        for n, act in enumerate((w_start, w_x, w_z, w_turn, w_x_back, w_core_back, w_end)):
            steps[f"w{n}_{j}"] = functools.partial(act, j)
    for name in ORDER:
        steps[name]()

    left(gp.at[pl.ds(0, 2)], ag_s.at[0])
    left(gp.at[3], ag_s.at[1])
    left(ps.at[2], rs_s.at[0])
    left(ps.at[pl.ds(0, 2)], rs_s.at[1])
    for n, (eight, zs) in enumerate(((f_rb, f_zb), (b_rb, b_zb))):
        left(eight.at[pl.ds(0, N_ROW - 1)], scan_s.at[n, 0])
        left(zs.at[pl.ds(0, N_Z - 1)], scan_s.at[n, 1])
        left(eight.at[pl.ds(0, N_ROW - 1)], scan_s.at[n, 2])
    left(wsend, w_s.at[0])
    left(xg, w_s.at[1])
    left(xs.at[:, pl.ds(0, N_X - 1)], w_s.at[2])
    left(xg.at[:, pl.ds(0, N_X - 1)], w_s.at[3])
    left(zsw.at[:, pl.ds(0, N_Z - 1)], w_s.at[4])
    left(zg.at[:, pl.ds(0, N_Z - 1)], w_s.at[5])


def write_out(*refs):
    sources, targets, done = refs[:5], refs[5:10], refs[10]
    copies = [
        pltpu.make_async_copy(a, b, done.at[i]) for i, (a, b) in enumerate(zip(sources, targets))
    ]
    for copy in copies:
        copy.start()
    for copy in copies:
        copy.wait()


def local(queries, attn_keys, attn_values, out_weight, grad_out, drop_seed):
    square = (ROWS, WIDTH)
    vmem = pltpu.VMEM
    scan_buffers = [
        vmem((8, 64, 128), BF16),
        vmem((8, 64, 128), BF16),
        vmem((64, 128), BF16),
        vmem((8, 64, 128), BF16),
        vmem((8, 64, 128), BF16),
        vmem((8, 64, 128), BF16),
    ]
    dma = pltpu.SemaphoreType.DMA
    scratch = [
        vmem(square, BF16), vmem(square, BF16), vmem(square, BF16), vmem(square, BF16),
        vmem((WIDTH, MODEL), BF16),
        vmem(square, F32),
        vmem((4,) + square, BF16),
        vmem((BLOCKS, HEADS, HD, HD), F32),
        vmem((BLOCKS * HEADS, SPAN, SPAN), BF16),
        vmem((BLOCKS * HEADS, HD, HD), BF16),
        vmem(square, F32),
        vmem(square, F32),
        vmem(square, BF16),
        vmem((WIDTH, ROWS), BF16),
        vmem((3,) + square, BF16),
        vmem(square, F32),
        vmem((2, BLOCKS, HALF, WIDTH), BF16),
        vmem((2,) + square, BF16),
        vmem(square, F32),
        vmem(square, BF16),
        vmem((BLOCKS, HEADS, HD, HD), F32),
        vmem(square, F32), vmem(square, F32),
        *scan_buffers, *scan_buffers,
        pltpu.SMEM((1,), jnp.int32),
        vmem((4, 256, 512), BF16),
        vmem((4, 256, 512), F32),
        vmem((4, 256, 512), BF16),
        vmem((4, 4, 64, 512), BF16),
        vmem((4, 4, 64, 512), BF16),
        vmem((4, 8, 16, 256), BF16),
        vmem((4, 8, 16, 256), BF16),
        vmem((4, 16, 256), BF16),
        vmem((4, 8, 16, 256), BF16),
        vmem((4, 4, 64, 512), BF16),
        vmem((4, 4, 64, 512), BF16),
        dma((6,)),
        dma((2,)), dma((7,)),
        dma((2,)), dma((6,)),
        dma((2, 3)), dma((2, 3)),
        dma((6,)), dma((6, 4)),
    ]
    hbm = pl.BlockSpec(memory_space=pl.ANY)
    outs = pl.pallas_call(
        kernel,
        out_shape=[vmem(square, BF16)] * 4 + [vmem((8, 64, MODEL), BF16)],
        in_specs=[hbm] * 6,
        out_specs=[pl.BlockSpec(memory_space=vmem)] * 5,
        scratch_shapes=scratch,
        compiler_params=pltpu.CompilerParams(
            collective_id=0, has_side_effects=True, vmem_limit_bytes=56 * 1024 * 1024
        ),
        cost_estimate=pl.CostEstimate(
            flops=7_000_000_000, bytes_accessed=11_000_000, transcendentals=3072
        ),
        name="layer",
    )(drop_seed, queries, attn_keys, attn_values, out_weight, grad_out)
    output, grad_q, grad_k, grad_v, grad_w = pl.pallas_call(
        write_out,
        out_shape=[jax.ShapeDtypeStruct(square, BF16)] * 4
        + [jax.ShapeDtypeStruct((8, 64, MODEL), BF16)],
        in_specs=[pl.BlockSpec(memory_space=vmem)] * 5,
        out_specs=[hbm] * 5,
        scratch_shapes=[dma((5,))],
        compiler_params=pltpu.CompilerParams(vmem_limit_bytes=1024 * 1024),
        name="write_out",
    )(*outs)
    return output, grad_q, grad_k, grad_v, grad_w.reshape(WIDTH, MODEL)


def solution(mesh):
    tokens = P("seq", "head")
    weight = P("head", None)
    return jax.shard_map(
        local,
        mesh=mesh,
        in_specs=(tokens, tokens, tokens, weight, tokens, P()),
        out_specs=(tokens, tokens, tokens, tokens, weight),
        check_vma=False,
    )
```

```python
import functools
import math

import jax
import jax.numpy as jnp
import numpy as np
from jax import lax
from jax.experimental import pallas as pl
from jax.experimental.pallas import tpu as pltpu
from jax.sharding import PartitionSpec as P

HD = 128
SPAN = 256
ROWS = 768
WIDTH = 512
MODEL = 2048
BLOCKS = ROWS // SPAN
HEADS = WIDTH // HD
N_ROW = 8
N_Z = 8
N_X = 4
HALF = SPAN // 2
EPS = 1e-05
KEEP_SCALE = 1.0 / 0.9
MODULUS = 32749.0
INVERSE = float(np.float32((1.0 - 2.0**-22) / 32749.0))
GRAD_SCALE = 1.0 / math.sqrt(49152)
MESH = pl.DeviceIdType.MESH
F32 = jnp.float32
BF16 = jnp.bfloat16

NN = (((1,), (0,)), ((), ()))
NT = (((1,), (1,)), ((), ()))
TN = (((0,), (0,)), ((), ()))


ORDER = (
    "go", "mask0", "states", "meet", "f1", "send0", "go_rest", "mask1", "send1", "mask2", "send2", "rest", "f2", "scores", "f3", "weight", "gn0",
    "relay0", "relay1", "relay2", "f4", "mix", "w0_0", "part_far", "part_next", "w1_0", "near", "w0_1", "w0_2", "gn1", "w1_1", "w1_2", "gn2", "own", "w2_0",
    "far0", "far1", "far2", "w0_3", "fill", "b1", "part_prev", "w2_1", "w2_2", "w3_0", "w1_3", "local0", "add0", "b2", "add1", "add2", "w3_1", "w3_2", "w4_0", "w2_3",
    "local1", "b3", "w4_1", "w4_2", "w5_0", "w3_3", "local2", "w6_0", "b4", "back_end", "w5_1", "w4_3", "w5_2", "w6_1", "w6_2", "fin0", "w5_3", "fin1", "fin2", "w6_3",
)


def dot(a, b, dims=NN):
    return lax.dot_general(a, b, dims, preferred_element_type=F32)


def wrap(value):
    quotient = jnp.floor(value * INVERSE)
    rest = value - quotient * MODULUS
    return jnp.where(rest >= MODULUS, rest - MODULUS, rest)


def keep_scales(positions, features, seed):
    mixing = wrap((positions * 181 + seed).astype(F32) + (features * 227).astype(F32))
    whole = mixing.astype(jnp.int32)
    square = whole * whole
    quotient = jnp.floor(square.astype(F32) * INVERSE).astype(jnp.int32)
    rest = square - quotient * 32749
    rest = jnp.where(rest >= 32749, rest - 32749, rest).astype(F32)
    offsets = (positions * 7).astype(F32) + (features * 13).astype(F32)
    hashed = wrap(rest * 173.0 + mixing * 59.0 + offsets)
    tens = jnp.floor((hashed + 0.5) * 0.1)
    return jnp.where(hashed - tens * 10.0 != 0.0, KEEP_SCALE, 0.0).astype(F32)


def rows(block):
    return pl.ds(block * SPAN, SPAN)


def half_rows(block, half):
    return pl.ds(block * SPAN + half * HALF, HALF)


def head(h):
    return pl.ds(h * HD, HD)


def kernel(
    seed_hbm, q_hbm, k_hbm, v_hbm, w_hbm, go_hbm,
    out_b, gq_b, gk_b, gv_b, gw_out,
    q, k, v, go, w, scale, gp, kv, cs, state, mixed, inv, normed, turned,
    ps, own, relay_in, rin, gn, gm, gkv, gk_acc, gv_acc,
    f_sb, f_rb, f_zs, f_zb, f_pb, f_fb, b_sb, b_rb, b_zs, b_zb, b_pb, b_fb,
    seed_ref, wsend, wown, wrecv, xs, xb, zsw, zbw, zone, zg, xg, pg,
    load_sem, ag_s, ag_r, rs_s, rs_r, scan_s, scan_r, w_s, w_r,
):
    seq = lax.axis_index("seq")
    y = lax.axis_index("head")
    z = seq // N_ROW
    r = seq % N_ROW
    x = r // 2
    c = r % 2
    other = 1 - c

    def at(zz, rr, yy):
        return {"seq": zz * N_ROW + rr, "head": yy}

    y_next, y_prev, y_far = (y + 1) % 4, (y + 3) % 4, (y + 2) % 4
    beside = (at(z, r, y_next), at(z, r, y_prev))
    partner = at(z, x * 2 + other, y)

    def row_peer(i):
        return (r + i) % N_ROW

    def z_peer(i):
        return (z + i) % N_Z

    def x_peer(i):
        return (x + i) % N_X

    def remote(src, dst, send, recv, device):
        return pltpu.make_async_remote_copy(
            src_ref=src, dst_ref=dst, send_sem=send, recv_sem=recv,
            device_id=device, device_id_type=MESH,
        )

    def loop(count, act):
        def step(i, _):
            act(i)
            return 0

        lax.fori_loop(1, count, step, 0)

    def start(copy):
        copy.start()

    def start_all(count, make):
        loop(count, lambda i: make(i).start())

    def arrive(ref, sem):
        remote(ref, ref, sem, sem, partner).wait_recv()

    def left(ref, sem):
        remote(ref, ref, sem, sem, partner).wait_send()

    barrier = pltpu.get_barrier_semaphore()
    for device in beside:
        pl.semaphore_signal(barrier, inc=1, device_id=device, device_id_type=MESH)

    def greet(i, _):
        pl.semaphore_signal(
            barrier, inc=1, device_id=at(z, row_peer(i), y), device_id_type=MESH
        )
        pl.semaphore_signal(
            barrier, inc=1, device_id=at(z_peer(i), r, y), device_id_type=MESH
        )
        return 0

    lax.fori_loop(1, N_ROW, greet, 0)

    rest = pl.ds(SPAN, ROWS - SPAN)
    loads = [
        pltpu.make_async_copy(a, b, load_sem.at[i])
        for i, (a, b) in enumerate(
            (
                (go_hbm.at[rows(0)], go.at[rows(0)]), (k_hbm, k), (v_hbm, v), (q_hbm, q),
                (w_hbm, w), (seed_hbm, seed_ref), (go_hbm.at[rest], go.at[rest]),
            )
        )
    ]
    for i in (5, 0, 1, 2, 6):
        loads[i].start()

    def ag_own(b, way, late):
        part = half_rows(b, 1 - way if late else way)
        return remote(
            gp.at[0, part], gp.at[1 + way, part], ag_s.at[0], ag_r.at[3 if late else b],
            beside[way],
        )

    def ag_relay(b, way):
        part = half_rows(b, way)
        return remote(
            gp.at[1 + way, part], gp.at[3, part], ag_s.at[1], ag_r.at[4 + b],
            beside[way],
        )

    first_row = seq * ROWS
    first_column = y * WIDTH
    features = first_column + lax.broadcasted_iota(jnp.int32, (1, WIDTH), 1)
    TILE = 32

    def mask(b):
        seed = seed_ref[0]

        def step(i, _):
            start = pl.multiple_of(b * SPAN + i * TILE, TILE)
            positions = first_row + start + lax.broadcasted_iota(jnp.int32, (TILE, 1), 0)
            kept = keep_scales(positions, features, seed)
            at_rows = pl.ds(start, TILE)
            scale[at_rows, :] = kept
            gp[0, at_rows, :] = (go[at_rows, :].astype(F32) * kept).astype(BF16)
            return 0

        lax.fori_loop(0, SPAN // TILE, step, 0)

    def block_states(b, _):
        at_rows = pl.ds(pl.multiple_of(b * SPAN, SPAN), SPAN)
        for h in range(HEADS):
            kv[b, h] = dot(k[at_rows, head(h)], v[at_rows, head(h)], TN)
        return 0

    def fill(sb, parts):
        for h in range(HEADS):
            total = (parts[0, h] + parts[1, h] + parts[2, h]).astype(BF16)
            sb[2 * h] = total[: HD // 2]
            sb[2 * h + 1] = total[HD // 2 :]

    def scan_one(n, i, sb, rb):
        t = row_peer(i)
        return remote(sb.at[t], rb.at[r], scan_s.at[n, 0], scan_r.at[n, 0], at(z, t, y))

    def scan_two(n, i, zs, zb):
        t = z_peer(i)
        return remote(zs, zb.at[z], scan_s.at[n, 1], scan_r.at[n, 1], at(t, r, y))

    def scan_three(n, i, pb, fb):
        t = row_peer(i)
        return remote(pb.at[t], fb.at[r], scan_s.at[n, 2], scan_r.at[n, 2], at(z, t, y))

    def scan_start(n, sb, rb):
        rb[r] = sb[r]
        start_all(N_ROW, lambda i: scan_one(n, i, sb, rb))

    def scan_middle(n, rb, zs, zb):
        arrive(rb.at[pl.ds(0, N_ROW - 1)], scan_r.at[n, 0])
        total = rb[0].astype(F32)
        for j in range(1, N_ROW):
            total = total + rb[j].astype(F32)
        total = total.astype(BF16)
        zs[...] = total
        zb[z] = total
        start_all(N_Z, lambda i: scan_two(n, i, zs, zb))

    def scan_late(n, rb, zb, pb, fb, reverse):
        arrive(zb.at[pl.ds(0, N_Z - 1)], scan_r.at[n, 1])
        run = jnp.zeros((HD // 2, HD), F32)
        for j in range(N_Z):
            wanted = (j > z) if reverse else (j < z)
            run = run + jnp.where(wanted, zb[j].astype(F32), 0.0)
        order = range(N_ROW - 1, -1, -1) if reverse else range(N_ROW)
        for j in order:
            pb[j] = run.astype(BF16)
            run = run + rb[j].astype(F32)
        fb[r] = pb[r]
        start_all(N_ROW, lambda i: scan_three(n, i, pb, fb))

    def scan_end(n, fb):
        arrive(fb.at[pl.ds(0, N_ROW - 1)], scan_r.at[n, 2])

    causal = lax.broadcasted_iota(jnp.int32, (SPAN, SPAN), 0) >= lax.broadcasted_iota(
        jnp.int32, (SPAN, SPAN), 1
    )

    def scores(b, _):
        at_rows = pl.ds(pl.multiple_of(b * SPAN, SPAN), SPAN)
        for h in range(HEADS):
            value = dot(q[at_rows, head(h)], k[at_rows, head(h)], NT)
            value = jnp.where(causal, value, 0.0).astype(BF16)
            cs[b * HEADS + h] = value
            mixed[at_rows, head(h)] = dot(value, v[at_rows, head(h)])
        return 0

    def columns(block):
        return pl.ds(pl.multiple_of(block * WIDTH, WIDTH), WIDTH)

    model_block = (y, y_prev, y_next, y_far)

    def add_grad_normed(slot, b):
        at_rows = pl.ds(pl.multiple_of(b * SPAN, SPAN), SPAN)
        term = dot(gp[slot, at_rows, :], w[:, columns(model_block[slot])], NT)
        gn[at_rows, :] = term if slot == 0 else gn[at_rows, :] + term

    def grad_normed(slot):
        def go_on(b, _):
            add_grad_normed(slot, b)
            return 0

        lax.fori_loop(0, BLOCKS, go_on, 0)

    def mix(b, _):
        at_rows = pl.ds(pl.multiple_of(b * SPAN, SPAN), SPAN)
        for h in range(HEADS):
            run = jnp.concatenate([f_fb[2 * h], f_fb[2 * h + 1]], axis=0).astype(F32)
            for earlier in range(BLOCKS - 1):
                run = run + jnp.where(earlier < b, kv[earlier, h], 0.0)
            held = run.astype(BF16)
            state[b * HEADS + h] = held
            value = mixed[at_rows, head(h)] + dot(q[at_rows, head(h)], held)
            mixed[at_rows, head(h)] = value
            power = jnp.sum(value * value, axis=1, keepdims=True) * (1.0 / HD)
            inverse = lax.rsqrt(power + EPS)
            inv[at_rows, head(h)] = jnp.broadcast_to(inverse, (SPAN, HD))
            normed[at_rows, head(h)] = (value * inverse).astype(BF16)
        turned[:, at_rows] = normed[at_rows, :].T
        return 0

    def rs_first(b, way):
        return remote(
            ps.at[2, half_rows(b, way)], relay_in.at[way, b],
            rs_s.at[0], rs_r.at[b], beside[way],
        )

    def rs_plain(b, way):
        part = half_rows(b, 1 - way)
        return remote(
            ps.at[way, part], rin.at[way, part], rs_s.at[1], rs_r.at[3 + b],
            beside[way],
        )

    def rs_added(b, way):
        part = half_rows(b, way)
        return remote(
            ps.at[way, part], rin.at[way, part], rs_s.at[1], rs_r.at[3 + b],
            beside[way],
        )

    def partial(slot, block):
        for b in range(BLOCKS):
            ps[slot, rows(b), :] = dot(normed[rows(b), :], w[:, columns(block)]).astype(BF16)
            if slot == 2:
                for way in range(2):
                    start(rs_first(b, way))
            else:
                start(rs_plain(b, slot))

    half = WIDTH // 2

    def core_out(j):
        return remote(wsend.at[j], wrecv.at[j], w_s.at[0], w_r.at[0, j], partner)

    def core_back(j):
        return remote(xg.at[j], pg.at[j], w_s.at[1], w_r.at[1, j], partner)

    def x_out(j, i):
        t = x_peer(i)
        return remote(
            xs.at[j, t], xb.at[j, x], w_s.at[2], w_r.at[2, j], at(z, t * 2 + c, y)
        )

    def x_back(j, i):
        t = x_peer(i)
        return remote(
            xg.at[j, x], xg.at[j, x], w_s.at[3], w_r.at[3, j], at(z, t * 2 + c, y)
        )

    def z_out(j, i):
        t = z_peer(i)
        return remote(
            zsw.at[j, t], zbw.at[j, z], w_s.at[4], w_r.at[4, j], at(t, r, y)
        )

    def z_back(j, i):
        t = z_peer(i)
        return remote(zone.at[j], zg.at[j, z], w_s.at[5], w_r.at[5, j], at(t, r, y))

    def w_start(j):
        theirs = pl.ds(pl.multiple_of(other * half, half), half)
        wsend[j] = dot(turned[theirs, :], gp[j]).astype(BF16)
        start(core_out(j))
        mine = pl.ds(pl.multiple_of(c * half, half), half)
        wown[j] = dot(turned[mine, :], gp[j])

    def w_x(j):
        arrive(wrecv.at[j], w_r.at[0, j])
        for t in range(N_X):
            part = pl.ds(t * 64, 64)
            xs[j, t] = (wown[j, part, :] + wrecv[j, part, :].astype(F32)).astype(BF16)
        xb[j, x] = xs[j, x]
        start_all(N_X, lambda i: x_out(j, i))

    def w_z(j):
        arrive(xb.at[j, pl.ds(0, N_X - 1)], w_r.at[2, j])
        total = xb[j, 0].astype(F32)
        for t in range(1, N_X):
            total = total + xb[j, t].astype(F32)
        total = total.astype(BF16)
        for t in range(N_Z):
            zsw[j, t] = total[(t // 2) * 16 : (t // 2) * 16 + 16, (t % 2) * 256 : (t % 2) * 256 + 256]
        zbw[j, z] = zsw[j, z]
        start_all(N_Z, lambda i: z_out(j, i))

    def w_turn(j):
        arrive(zbw.at[j, pl.ds(0, N_Z - 1)], w_r.at[4, j])
        total = zbw[j, 0].astype(F32)
        for t in range(1, N_Z):
            total = total + zbw[j, t].astype(F32)
        total = (total * GRAD_SCALE).astype(BF16)
        zone[j] = total
        zg[j, z] = total
        start_all(N_Z, lambda i: z_back(j, i))

    def w_x_back(j):
        arrive(zg.at[j, pl.ds(0, N_Z - 1)], w_r.at[5, j])
        pieces = [
            jnp.concatenate([zg[j, 2 * t], zg[j, 2 * t + 1]], axis=1) for t in range(N_Z // 2)
        ]
        xg[j, x] = jnp.concatenate(pieces, axis=0)
        start_all(N_X, lambda i: x_back(j, i))

    def w_store(j, own_half):
        source = xg if own_half else pg
        first = (c if own_half else other) * N_X
        for t in range(N_X):
            gw_out[first + t, :, columns(model_block[j])] = source[j, t]

    def w_core_back(j):
        arrive(xg.at[j, pl.ds(0, N_X - 1)], w_r.at[3, j])
        start(core_back(j))
        w_store(j, True)

    def w_end(j):
        arrive(pg.at[j], w_r.at[1, j])
        w_store(j, False)

    def back_mix(b, _):
        at_rows = pl.ds(pl.multiple_of(b * SPAN, SPAN), SPAN)
        for h in range(HEADS):
            grad = gn[at_rows, head(h)]
            value = mixed[at_rows, head(h)]
            inverse = inv[at_rows, head(h)]
            mean = jnp.sum(grad * value, axis=1, keepdims=True) * (1.0 / HD)
            held = (inverse * (grad - value * inverse * inverse * mean)).astype(BF16)
            gm[at_rows, head(h)] = held
            gkv[b, h] = dot(q[at_rows, head(h)], held, TN)
        return 0

    def add_relayed(b):
        arrive(relay_in.at[:, b], rs_r.at[b])
        for way in range(2):
            part = half_rows(b, way)
            both = ps[way, part, :].astype(F32) + relay_in[way, b].astype(F32)
            ps[way, part, :] = both.astype(BF16)
            start(rs_added(b, way))

    def back_local(b, _):
        at_rows = pl.ds(pl.multiple_of(b * SPAN, SPAN), SPAN)
        for h in range(HEADS):
            grad = gm[at_rows, head(h)]
            gs = dot(grad, v[at_rows, head(h)], NT)
            gs = jnp.where(causal, gs, 0.0).astype(BF16)
            gq_b[at_rows, head(h)] = (
                dot(grad, state[b * HEADS + h], NT) + dot(gs, k[at_rows, head(h)])
            ).astype(BF16)
            gk_acc[at_rows, head(h)] = dot(gs, q[at_rows, head(h)], TN)
            gv_acc[at_rows, head(h)] = dot(cs[b * HEADS + h], grad, TN)
        return 0

    def back_end(b, _):
        at_rows = pl.ds(pl.multiple_of(b * SPAN, SPAN), SPAN)
        for h in range(HEADS):
            run = jnp.concatenate([b_fb[2 * h], b_fb[2 * h + 1]], axis=0).astype(F32)
            for later in range(1, BLOCKS):
                run = run + jnp.where(later > b, gkv[later, h], 0.0)
            held = run.astype(BF16)
            gk_b[at_rows, head(h)] = (
                gk_acc[at_rows, head(h)] + dot(v[at_rows, head(h)], held, NT)
            ).astype(BF16)
            gv_b[at_rows, head(h)] = (
                gv_acc[at_rows, head(h)] + dot(k[at_rows, head(h)], held)
            ).astype(BF16)
        return 0

    def finish(b):
        arrive(rin.at[:, rows(b)], rs_r.at[3 + b])

        def step(i, _):
            at_rows = pl.ds(pl.multiple_of(b * SPAN + i * 32, 32), 32)
            total = own[at_rows, :] + rin[0, at_rows, :].astype(F32) + rin[1, at_rows, :].astype(F32)
            out_b[at_rows, :] = (total * scale[at_rows, :]).astype(BF16)
            return 0

        lax.fori_loop(0, SPAN // 32, step, 0)

    def blocks(body):
        lax.fori_loop(0, BLOCKS, body, 0)

    def do_send(b):
        for way in range(2):
            start(ag_own(b, way, 0))

    def do_rest():
        for b in range(BLOCKS):
            for way in range(2):
                start(ag_own(b, way, 1))

    def do_relay(b):
        arrive(gp.at[1, rows(b)], ag_r.at[b])
        for way in range(2):
            start(ag_relay(b, way))

    def do_near():
        arrive(gp.at[1], ag_r.at[3])

    def do_far(b):
        arrive(gp.at[3, rows(b)], ag_r.at[4 + b])

    def do_go():
        loads[5].wait()
        loads[0].wait()
        loads[3].start()
        loads[4].start()

    def do_states():
        loads[1].wait()
        loads[2].wait()
        blocks(block_states)
        fill(f_sb, kv)

    def do_scores():
        loads[3].wait()
        blocks(scores)

    def do_own():
        for b in range(BLOCKS):
            own[rows(b), :] = dot(normed[rows(b), :], w[:, columns(y)])

    def do_far_mix(b):
        do_far(b)
        add_grad_normed(3, b)
        back_mix(b, 0)

    def do_back_end():
        blocks(back_end)

    steps = {
        "go": do_go,
        "go_rest": loads[6].wait,
        "weight": loads[4].wait,
        "meet": lambda: pl.semaphore_wait(barrier, 2 + N_ROW - 1 + N_Z - 1),
        "states": do_states,
        "scores": do_scores,
        "mix": lambda: blocks(mix),
        "rest": do_rest,
        "near": do_near,
        "fill": lambda: fill(b_sb, gkv),
        "back_end": do_back_end,
        "own": do_own,
        "part_far": lambda: partial(2, y_far),
        "part_next": lambda: partial(0, y_next),
        "part_prev": lambda: partial(1, y_prev),
        "f1": lambda: scan_start(0, f_sb, f_rb),
        "f2": lambda: scan_middle(0, f_rb, f_zs, f_zb),
        "f3": lambda: scan_late(0, f_rb, f_zb, f_pb, f_fb, False),
        "f4": lambda: scan_end(0, f_fb),
        "b1": lambda: scan_start(1, b_sb, b_rb),
        "b2": lambda: scan_middle(1, b_rb, b_zs, b_zb),
        "b3": lambda: scan_late(1, b_rb, b_zb, b_pb, b_fb, True),
        "b4": lambda: scan_end(1, b_fb),
    }
    for b in range(BLOCKS):
        steps[f"mask{b}"] = functools.partial(mask, b)
        steps[f"send{b}"] = functools.partial(do_send, b)
        steps[f"relay{b}"] = functools.partial(do_relay, b)
        steps[f"add{b}"] = functools.partial(add_relayed, b)
        steps[f"local{b}"] = functools.partial(back_local, b, 0)
        steps[f"fin{b}"] = functools.partial(finish, b)
        steps[f"far{b}"] = functools.partial(do_far_mix, b)
    for j in range(4):
        steps[f"gn{j}"] = functools.partial(grad_normed, j)
        for n, act in enumerate((w_start, w_x, w_z, w_turn, w_x_back, w_core_back, w_end)):
            steps[f"w{n}_{j}"] = functools.partial(act, j)
    for name in ORDER:
        steps[name]()

    left(gp.at[pl.ds(0, 2)], ag_s.at[0])
    left(gp.at[3], ag_s.at[1])
    left(ps.at[2], rs_s.at[0])
    left(ps.at[pl.ds(0, 2)], rs_s.at[1])
    for n, (eight, zs) in enumerate(((f_rb, f_zb), (b_rb, b_zb))):
        left(eight.at[pl.ds(0, N_ROW - 1)], scan_s.at[n, 0])
        left(zs.at[pl.ds(0, N_Z - 1)], scan_s.at[n, 1])
        left(eight.at[pl.ds(0, N_ROW - 1)], scan_s.at[n, 2])
    left(wsend, w_s.at[0])
    left(xg, w_s.at[1])
    left(xs.at[:, pl.ds(0, N_X - 1)], w_s.at[2])
    left(xg.at[:, pl.ds(0, N_X - 1)], w_s.at[3])
    left(zsw.at[:, pl.ds(0, N_Z - 1)], w_s.at[4])
    left(zg.at[:, pl.ds(0, N_Z - 1)], w_s.at[5])


def write_out(*refs):
    sources, targets, done = refs[:5], refs[5:10], refs[10]
    for i, (source, target) in enumerate(zip(sources, targets)):
        part = source.shape[0] // 4
        for n in range(4):
            at = pl.ds(n * part, part)
            pltpu.make_async_copy(source.at[at], target.at[at], done.at[i]).start()
    for i, (source, target) in enumerate(zip(sources, targets)):
        pltpu.make_async_copy(source, target, done.at[i]).wait()


def local(queries, attn_keys, attn_values, out_weight, grad_out, drop_seed):
    square = (ROWS, WIDTH)
    vmem = pltpu.VMEM
    scan_buffers = [
        vmem((8, 64, 128), BF16),
        vmem((8, 64, 128), BF16),
        vmem((64, 128), BF16),
        vmem((8, 64, 128), BF16),
        vmem((8, 64, 128), BF16),
        vmem((8, 64, 128), BF16),
    ]
    dma = pltpu.SemaphoreType.DMA
    scratch = [
        vmem(square, BF16), vmem(square, BF16), vmem(square, BF16), vmem(square, BF16),
        vmem((WIDTH, MODEL), BF16),
        vmem(square, F32),
        vmem((4,) + square, BF16),
        vmem((BLOCKS, HEADS, HD, HD), F32),
        vmem((BLOCKS * HEADS, SPAN, SPAN), BF16),
        vmem((BLOCKS * HEADS, HD, HD), BF16),
        vmem(square, F32),
        vmem(square, F32),
        vmem(square, BF16),
        vmem((WIDTH, ROWS), BF16),
        vmem((3,) + square, BF16),
        vmem(square, F32),
        vmem((2, BLOCKS, HALF, WIDTH), BF16),
        vmem((2,) + square, BF16),
        vmem(square, F32),
        vmem(square, BF16),
        vmem((BLOCKS, HEADS, HD, HD), F32),
        vmem(square, F32), vmem(square, F32),
        *scan_buffers, *scan_buffers,
        pltpu.SMEM((1,), jnp.int32),
        vmem((4, 256, 512), BF16),
        vmem((4, 256, 512), F32),
        vmem((4, 256, 512), BF16),
        vmem((4, 4, 64, 512), BF16),
        vmem((4, 4, 64, 512), BF16),
        vmem((4, 8, 16, 256), BF16),
        vmem((4, 8, 16, 256), BF16),
        vmem((4, 16, 256), BF16),
        vmem((4, 8, 16, 256), BF16),
        vmem((4, 4, 64, 512), BF16),
        vmem((4, 4, 64, 512), BF16),
        dma((7,)),
        dma((2,)), dma((7,)),
        dma((2,)), dma((6,)),
        dma((2, 3)), dma((2, 3)),
        dma((6,)), dma((6, 4)),
    ]
    hbm = pl.BlockSpec(memory_space=pl.ANY)
    outs = pl.pallas_call(
        kernel,
        out_shape=[vmem(square, BF16)] * 4 + [vmem((8, 64, MODEL), BF16)],
        in_specs=[hbm] * 6,
        out_specs=[pl.BlockSpec(memory_space=vmem)] * 5,
        scratch_shapes=scratch,
        compiler_params=pltpu.CompilerParams(
            collective_id=0, has_side_effects=True, vmem_limit_bytes=56 * 1024 * 1024
        ),
        cost_estimate=pl.CostEstimate(
            flops=7_000_000_000, bytes_accessed=11_000_000, transcendentals=3072
        ),
        name="layer",
    )(drop_seed, queries, attn_keys, attn_values, out_weight, grad_out)
    output, grad_q, grad_k, grad_v, grad_w = pl.pallas_call(
        write_out,
        out_shape=[jax.ShapeDtypeStruct(square, BF16)] * 4
        + [jax.ShapeDtypeStruct((8, 64, MODEL), BF16)],
        in_specs=[pl.BlockSpec(memory_space=vmem)] * 5,
        out_specs=[hbm] * 5,
        scratch_shapes=[dma((5,))],
        compiler_params=pltpu.CompilerParams(vmem_limit_bytes=1024 * 1024),
        name="write_out",
    )(*outs)
    return output, grad_q, grad_k, grad_v, grad_w.reshape(WIDTH, MODEL)


def solution(mesh):
    tokens = P("seq", "head")
    weight = P("head", None)
    return jax.shard_map(
        local,
        mesh=mesh,
        in_specs=(tokens, tokens, tokens, weight, tokens, P()),
        out_specs=(tokens, tokens, tokens, tokens, weight),
        check_vma=False,
    )
```

```python
import functools
import math

import jax
import jax.numpy as jnp
import numpy as np
from jax import lax
from jax.experimental import pallas as pl
from jax.experimental.pallas import tpu as pltpu
from jax.sharding import PartitionSpec as P

HD = 128
SPAN = 256
ROWS = 768
WIDTH = 512
MODEL = 2048
BLOCKS = ROWS // SPAN
HEADS = WIDTH // HD
N_ROW = 8
N_Z = 8
N_X = 4
HALF = SPAN // 2
EPS = 1e-05
KEEP_SCALE = 1.0 / 0.9
MODULUS = 32749.0
INVERSE = float(np.float32((1.0 - 2.0**-22) / 32749.0))
GRAD_SCALE = 1.0 / math.sqrt(49152)
MESH = pl.DeviceIdType.MESH
F32 = jnp.float32
BF16 = jnp.bfloat16

NN = (((1,), (0,)), ((), ()))
NT = (((1,), (1,)), ((), ()))
TN = (((0,), (0,)), ((), ()))


ORDER = (
    "go", "mask0", "states", "meet", "f1", "send0", "go_rest", "mask1", "send1", "mask2", "send2", "rest", "f2", "scores", "f3", "weight", "gn0",
    "relay0", "relay1", "relay2", "f4", "mix", "w0_0", "part_far", "part_next", "w1_0", "near", "w0_1", "w0_2", "gn1", "w1_1", "w1_2", "gn2", "own", "w2_0",
    "far0", "far1", "far2", "w0_3", "fill", "b1", "part_prev", "w2_1", "w2_2", "w3_0", "w1_3", "local0", "add0", "b2", "add1", "add2", "w3_1", "w3_2", "w4_0", "w2_3",
    "local1", "b3", "w4_1", "w4_2", "w5_0", "w3_3", "local2", "w6_0", "b4", "back_end", "w5_1", "w4_3", "w5_2", "w6_1", "w6_2", "fin0", "w5_3", "fin1", "fin2", "w6_3",
)


def dot(a, b, dims=NN):
    return lax.dot_general(a, b, dims, preferred_element_type=F32)


def wrap(value):
    quotient = jnp.floor(value * INVERSE)
    rest = value - quotient * MODULUS
    return jnp.where(rest >= MODULUS, rest - MODULUS, rest)


def keep_scales(positions, features, seed):
    mixing = wrap((positions * 181 + seed).astype(F32) + (features * 227).astype(F32))
    whole = mixing.astype(jnp.int32)
    square = whole * whole
    quotient = jnp.floor(square.astype(F32) * INVERSE).astype(jnp.int32)
    rest = square - quotient * 32749
    rest = jnp.where(rest >= 32749, rest - 32749, rest).astype(F32)
    offsets = (positions * 7).astype(F32) + (features * 13).astype(F32)
    hashed = wrap(rest * 173.0 + mixing * 59.0 + offsets)
    tens = jnp.floor((hashed + 0.5) * 0.1)
    return jnp.where(hashed - tens * 10.0 != 0.0, KEEP_SCALE, 0.0).astype(F32)


def rows(block):
    return pl.ds(block * SPAN, SPAN)


def half_rows(block, half):
    return pl.ds(block * SPAN + half * HALF, HALF)


def head(h):
    return pl.ds(h * HD, HD)


def kernel(
    seed_hbm, q_hbm, k_hbm, v_hbm, w_hbm, go_hbm,
    out_b, gq_b, gk_b, gv_b, gw_out,
    q, k, v, go, w, scale, gp, kv, cs, state, mixed, inv, normed, turned,
    ps, own, relay_in, rin, gn, gm, gkv, gk_acc, gv_acc,
    f_sb, f_rb, f_zs, f_zb, f_pb, f_fb, b_sb, b_rb, b_zs, b_zb, b_pb, b_fb,
    seed_ref, wsend, wown, wrecv, xs, xb, zsw, zbw, zone, zg, xg, pg,
    load_sem, ag_s, ag_r, rs_s, rs_r, scan_s, scan_r, w_s, w_r,
):
    seq = lax.axis_index("seq")
    y = lax.axis_index("head")
    z = seq // N_ROW
    r = seq % N_ROW
    x = r // 2
    c = r % 2
    other = 1 - c

    def at(zz, rr, yy):
        return {"seq": zz * N_ROW + rr, "head": yy}

    y_next, y_prev, y_far = (y + 1) % 4, (y + 3) % 4, (y + 2) % 4
    beside = (at(z, r, y_next), at(z, r, y_prev))
    partner = at(z, x * 2 + other, y)

    def row_peer(i):
        return (r + i) % N_ROW

    def z_peer(i):
        return (z + i) % N_Z

    def x_peer(i):
        return (x + i) % N_X

    def remote(src, dst, send, recv, device):
        return pltpu.make_async_remote_copy(
            src_ref=src, dst_ref=dst, send_sem=send, recv_sem=recv,
            device_id=device, device_id_type=MESH,
        )

    def loop(count, act):
        def step(i, _):
            act((i + count // 2 - 2) % (count - 1) + 1)
            return 0

        lax.fori_loop(1, count, step, 0)

    def start(copy):
        copy.start()

    def start_all(count, make):
        loop(count, lambda i: make(i).start())

    def arrive(ref, sem):
        remote(ref, ref, sem, sem, partner).wait_recv()

    def left(ref, sem):
        remote(ref, ref, sem, sem, partner).wait_send()

    barrier = pltpu.get_barrier_semaphore()
    for device in beside:
        pl.semaphore_signal(barrier, inc=1, device_id=device, device_id_type=MESH)

    def greet(i, _):
        pl.semaphore_signal(
            barrier, inc=1, device_id=at(z, row_peer(i), y), device_id_type=MESH
        )
        pl.semaphore_signal(
            barrier, inc=1, device_id=at(z_peer(i), r, y), device_id_type=MESH
        )
        return 0

    lax.fori_loop(1, N_ROW, greet, 0)

    rest = pl.ds(SPAN, ROWS - SPAN)
    loads = [
        pltpu.make_async_copy(a, b, load_sem.at[i])
        for i, (a, b) in enumerate(
            (
                (go_hbm.at[rows(0)], go.at[rows(0)]), (k_hbm, k), (v_hbm, v), (q_hbm, q),
                (w_hbm, w), (seed_hbm, seed_ref), (go_hbm.at[rest], go.at[rest]),
            )
        )
    ]
    for i in (5, 0, 1, 2, 6):
        loads[i].start()

    def ag_own(b, way, late):
        part = half_rows(b, 1 - way if late else way)
        return remote(
            gp.at[0, part], gp.at[1 + way, part], ag_s.at[0], ag_r.at[3 if late else b],
            beside[way],
        )

    def ag_relay(b, way):
        part = half_rows(b, way)
        return remote(
            gp.at[1 + way, part], gp.at[3, part], ag_s.at[1], ag_r.at[4 + b],
            beside[way],
        )

    first_row = seq * ROWS
    first_column = y * WIDTH
    features = first_column + lax.broadcasted_iota(jnp.int32, (1, WIDTH), 1)
    TILE = 32

    def mask(b):
        seed = seed_ref[0]

        def step(i, _):
            start = pl.multiple_of(b * SPAN + i * TILE, TILE)
            positions = first_row + start + lax.broadcasted_iota(jnp.int32, (TILE, 1), 0)
            kept = keep_scales(positions, features, seed)
            at_rows = pl.ds(start, TILE)
            scale[at_rows, :] = kept
            gp[0, at_rows, :] = (go[at_rows, :].astype(F32) * kept).astype(BF16)
            return 0

        lax.fori_loop(0, SPAN // TILE, step, 0)

    def block_states(b, _):
        at_rows = pl.ds(pl.multiple_of(b * SPAN, SPAN), SPAN)
        for h in range(HEADS):
            kv[b, h] = dot(k[at_rows, head(h)], v[at_rows, head(h)], TN)
        return 0

    def fill(sb, parts):
        for h in range(HEADS):
            total = (parts[0, h] + parts[1, h] + parts[2, h]).astype(BF16)
            sb[2 * h] = total[: HD // 2]
            sb[2 * h + 1] = total[HD // 2 :]

    def scan_one(n, i, sb, rb):
        t = row_peer(i)
        return remote(sb.at[t], rb.at[r], scan_s.at[n, 0], scan_r.at[n, 0], at(z, t, y))

    def scan_two(n, i, zs, zb):
        t = z_peer(i)
        return remote(zs, zb.at[z], scan_s.at[n, 1], scan_r.at[n, 1], at(t, r, y))

    def scan_three(n, i, pb, fb):
        t = row_peer(i)
        return remote(pb.at[t], fb.at[r], scan_s.at[n, 2], scan_r.at[n, 2], at(z, t, y))

    def scan_start(n, sb, rb):
        rb[r] = sb[r]
        start_all(N_ROW, lambda i: scan_one(n, i, sb, rb))

    def scan_middle(n, rb, zs, zb):
        arrive(rb.at[pl.ds(0, N_ROW - 1)], scan_r.at[n, 0])
        total = rb[0].astype(F32)
        for j in range(1, N_ROW):
            total = total + rb[j].astype(F32)
        total = total.astype(BF16)
        zs[...] = total
        zb[z] = total
        start_all(N_Z, lambda i: scan_two(n, i, zs, zb))

    def scan_late(n, rb, zb, pb, fb, reverse):
        arrive(zb.at[pl.ds(0, N_Z - 1)], scan_r.at[n, 1])
        run = jnp.zeros((HD // 2, HD), F32)
        for j in range(N_Z):
            wanted = (j > z) if reverse else (j < z)
            run = run + jnp.where(wanted, zb[j].astype(F32), 0.0)
        order = range(N_ROW - 1, -1, -1) if reverse else range(N_ROW)
        for j in order:
            pb[j] = run.astype(BF16)
            run = run + rb[j].astype(F32)
        fb[r] = pb[r]
        start_all(N_ROW, lambda i: scan_three(n, i, pb, fb))

    def scan_end(n, fb):
        arrive(fb.at[pl.ds(0, N_ROW - 1)], scan_r.at[n, 2])

    causal = lax.broadcasted_iota(jnp.int32, (SPAN, SPAN), 0) >= lax.broadcasted_iota(
        jnp.int32, (SPAN, SPAN), 1
    )

    def scores(b, _):
        at_rows = pl.ds(pl.multiple_of(b * SPAN, SPAN), SPAN)
        for h in range(HEADS):
            value = dot(q[at_rows, head(h)], k[at_rows, head(h)], NT)
            value = jnp.where(causal, value, 0.0).astype(BF16)
            cs[b * HEADS + h] = value
            mixed[at_rows, head(h)] = dot(value, v[at_rows, head(h)])
        return 0

    def columns(block):
        return pl.ds(pl.multiple_of(block * WIDTH, WIDTH), WIDTH)

    model_block = (y, y_prev, y_next, y_far)

    def add_grad_normed(slot, b):
        at_rows = pl.ds(pl.multiple_of(b * SPAN, SPAN), SPAN)
        term = dot(gp[slot, at_rows, :], w[:, columns(model_block[slot])], NT)
        gn[at_rows, :] = term if slot == 0 else gn[at_rows, :] + term

    def grad_normed(slot):
        def go_on(b, _):
            add_grad_normed(slot, b)
            return 0

        lax.fori_loop(0, BLOCKS, go_on, 0)

    def mix(b, _):
        at_rows = pl.ds(pl.multiple_of(b * SPAN, SPAN), SPAN)
        for h in range(HEADS):
            run = jnp.concatenate([f_fb[2 * h], f_fb[2 * h + 1]], axis=0).astype(F32)
            for earlier in range(BLOCKS - 1):
                run = run + jnp.where(earlier < b, kv[earlier, h], 0.0)
            held = run.astype(BF16)
            state[b * HEADS + h] = held
            value = mixed[at_rows, head(h)] + dot(q[at_rows, head(h)], held)
            mixed[at_rows, head(h)] = value
            power = jnp.sum(value * value, axis=1, keepdims=True) * (1.0 / HD)
            inverse = lax.rsqrt(power + EPS)
            inv[at_rows, head(h)] = jnp.broadcast_to(inverse, (SPAN, HD))
            normed[at_rows, head(h)] = (value * inverse).astype(BF16)
        turned[:, at_rows] = normed[at_rows, :].T
        return 0

    def rs_first(b, way):
        return remote(
            ps.at[2, half_rows(b, way)], relay_in.at[way, b],
            rs_s.at[0], rs_r.at[b], beside[way],
        )

    def rs_plain(b, way):
        part = half_rows(b, 1 - way)
        return remote(
            ps.at[way, part], rin.at[way, part], rs_s.at[1], rs_r.at[3 + b],
            beside[way],
        )

    def rs_added(b, way):
        part = half_rows(b, way)
        return remote(
            ps.at[way, part], rin.at[way, part], rs_s.at[1], rs_r.at[3 + b],
            beside[way],
        )

    def partial(slot, block):
        for b in range(BLOCKS):
            ps[slot, rows(b), :] = dot(normed[rows(b), :], w[:, columns(block)]).astype(BF16)
            if slot == 2:
                for way in range(2):
                    start(rs_first(b, way))
            else:
                start(rs_plain(b, slot))

    half = WIDTH // 2

    def core_out(j):
        return remote(wsend.at[j], wrecv.at[j], w_s.at[0], w_r.at[0, j], partner)

    def core_back(j):
        return remote(xg.at[j], pg.at[j], w_s.at[1], w_r.at[1, j], partner)

    def x_out(j, i):
        t = x_peer(i)
        return remote(
            xs.at[j, t], xb.at[j, x], w_s.at[2], w_r.at[2, j], at(z, t * 2 + c, y)
        )

    def x_back(j, i):
        t = x_peer(i)
        return remote(
            xg.at[j, x], xg.at[j, x], w_s.at[3], w_r.at[3, j], at(z, t * 2 + c, y)
        )

    def z_out(j, i):
        t = z_peer(i)
        return remote(
            zsw.at[j, t], zbw.at[j, z], w_s.at[4], w_r.at[4, j], at(t, r, y)
        )

    def z_back(j, i):
        t = z_peer(i)
        return remote(zone.at[j], zg.at[j, z], w_s.at[5], w_r.at[5, j], at(t, r, y))

    def w_start(j):
        theirs = pl.ds(pl.multiple_of(other * half, half), half)
        wsend[j] = dot(turned[theirs, :], gp[j]).astype(BF16)
        start(core_out(j))
        mine = pl.ds(pl.multiple_of(c * half, half), half)
        wown[j] = dot(turned[mine, :], gp[j])

    def w_x(j):
        arrive(wrecv.at[j], w_r.at[0, j])
        for t in range(N_X):
            part = pl.ds(t * 64, 64)
            xs[j, t] = (wown[j, part, :] + wrecv[j, part, :].astype(F32)).astype(BF16)
        xb[j, x] = xs[j, x]
        start_all(N_X, lambda i: x_out(j, i))

    def w_z(j):
        arrive(xb.at[j, pl.ds(0, N_X - 1)], w_r.at[2, j])
        total = xb[j, 0].astype(F32)
        for t in range(1, N_X):
            total = total + xb[j, t].astype(F32)
        total = total.astype(BF16)
        for t in range(N_Z):
            zsw[j, t] = total[(t // 2) * 16 : (t // 2) * 16 + 16, (t % 2) * 256 : (t % 2) * 256 + 256]
        zbw[j, z] = zsw[j, z]
        start_all(N_Z, lambda i: z_out(j, i))

    def w_turn(j):
        arrive(zbw.at[j, pl.ds(0, N_Z - 1)], w_r.at[4, j])
        total = zbw[j, 0].astype(F32)
        for t in range(1, N_Z):
            total = total + zbw[j, t].astype(F32)
        total = (total * GRAD_SCALE).astype(BF16)
        zone[j] = total
        zg[j, z] = total
        start_all(N_Z, lambda i: z_back(j, i))

    def w_x_back(j):
        arrive(zg.at[j, pl.ds(0, N_Z - 1)], w_r.at[5, j])
        pieces = [
            jnp.concatenate([zg[j, 2 * t], zg[j, 2 * t + 1]], axis=1) for t in range(N_Z // 2)
        ]
        xg[j, x] = jnp.concatenate(pieces, axis=0)
        start_all(N_X, lambda i: x_back(j, i))

    def w_store(j, own_half):
        source = xg if own_half else pg
        first = (c if own_half else other) * N_X
        for t in range(N_X):
            gw_out[first + t, :, columns(model_block[j])] = source[j, t]

    def w_core_back(j):
        arrive(xg.at[j, pl.ds(0, N_X - 1)], w_r.at[3, j])
        start(core_back(j))
        w_store(j, True)

    def w_end(j):
        arrive(pg.at[j], w_r.at[1, j])
        w_store(j, False)

    def back_mix(b, _):
        at_rows = pl.ds(pl.multiple_of(b * SPAN, SPAN), SPAN)
        for h in range(HEADS):
            grad = gn[at_rows, head(h)]
            value = mixed[at_rows, head(h)]
            inverse = inv[at_rows, head(h)]
            mean = jnp.sum(grad * value, axis=1, keepdims=True) * (1.0 / HD)
            held = (inverse * (grad - value * inverse * inverse * mean)).astype(BF16)
            gm[at_rows, head(h)] = held
            gkv[b, h] = dot(q[at_rows, head(h)], held, TN)
        return 0

    def add_relayed(b):
        arrive(relay_in.at[:, b], rs_r.at[b])
        for way in range(2):
            part = half_rows(b, way)
            both = ps[way, part, :].astype(F32) + relay_in[way, b].astype(F32)
            ps[way, part, :] = both.astype(BF16)
            start(rs_added(b, way))

    def back_local(b, _):
        at_rows = pl.ds(pl.multiple_of(b * SPAN, SPAN), SPAN)
        for h in range(HEADS):
            grad = gm[at_rows, head(h)]
            gs = dot(grad, v[at_rows, head(h)], NT)
            gs = jnp.where(causal, gs, 0.0).astype(BF16)
            gq_b[at_rows, head(h)] = (
                dot(grad, state[b * HEADS + h], NT) + dot(gs, k[at_rows, head(h)])
            ).astype(BF16)
            gk_acc[at_rows, head(h)] = dot(gs, q[at_rows, head(h)], TN)
            gv_acc[at_rows, head(h)] = dot(cs[b * HEADS + h], grad, TN)
        return 0

    def back_end(b, _):
        at_rows = pl.ds(pl.multiple_of(b * SPAN, SPAN), SPAN)
        for h in range(HEADS):
            run = jnp.concatenate([b_fb[2 * h], b_fb[2 * h + 1]], axis=0).astype(F32)
            for later in range(1, BLOCKS):
                run = run + jnp.where(later > b, gkv[later, h], 0.0)
            held = run.astype(BF16)
            gk_b[at_rows, head(h)] = (
                gk_acc[at_rows, head(h)] + dot(v[at_rows, head(h)], held, NT)
            ).astype(BF16)
            gv_b[at_rows, head(h)] = (
                gv_acc[at_rows, head(h)] + dot(k[at_rows, head(h)], held)
            ).astype(BF16)
        return 0

    def finish(b):
        arrive(rin.at[:, rows(b)], rs_r.at[3 + b])

        def step(i, _):
            at_rows = pl.ds(pl.multiple_of(b * SPAN + i * 32, 32), 32)
            total = own[at_rows, :] + rin[0, at_rows, :].astype(F32) + rin[1, at_rows, :].astype(F32)
            out_b[at_rows, :] = (total * scale[at_rows, :]).astype(BF16)
            return 0

        lax.fori_loop(0, SPAN // 32, step, 0)

    def blocks(body):
        lax.fori_loop(0, BLOCKS, body, 0)

    def do_send(b):
        for way in range(2):
            start(ag_own(b, way, 0))

    def do_rest():
        for b in range(BLOCKS):
            for way in range(2):
                start(ag_own(b, way, 1))

    def do_relay(b):
        arrive(gp.at[1, rows(b)], ag_r.at[b])
        for way in range(2):
            start(ag_relay(b, way))

    def do_near():
        arrive(gp.at[1], ag_r.at[3])

    def do_far(b):
        arrive(gp.at[3, rows(b)], ag_r.at[4 + b])

    def do_go():
        loads[5].wait()
        loads[0].wait()
        loads[3].start()
        loads[4].start()

    def do_states():
        loads[1].wait()
        loads[2].wait()
        blocks(block_states)
        fill(f_sb, kv)

    def do_scores():
        loads[3].wait()
        blocks(scores)

    def do_own():
        for b in range(BLOCKS):
            own[rows(b), :] = dot(normed[rows(b), :], w[:, columns(y)])

    def do_far_mix(b):
        do_far(b)
        add_grad_normed(3, b)
        back_mix(b, 0)

    def do_back_end():
        blocks(back_end)

    steps = {
        "go": do_go,
        "go_rest": loads[6].wait,
        "weight": loads[4].wait,
        "meet": lambda: pl.semaphore_wait(barrier, 2 + N_ROW - 1 + N_Z - 1),
        "states": do_states,
        "scores": do_scores,
        "mix": lambda: blocks(mix),
        "rest": do_rest,
        "near": do_near,
        "fill": lambda: fill(b_sb, gkv),
        "back_end": do_back_end,
        "own": do_own,
        "part_far": lambda: partial(2, y_far),
        "part_next": lambda: partial(0, y_next),
        "part_prev": lambda: partial(1, y_prev),
        "f1": lambda: scan_start(0, f_sb, f_rb),
        "f2": lambda: scan_middle(0, f_rb, f_zs, f_zb),
        "f3": lambda: scan_late(0, f_rb, f_zb, f_pb, f_fb, False),
        "f4": lambda: scan_end(0, f_fb),
        "b1": lambda: scan_start(1, b_sb, b_rb),
        "b2": lambda: scan_middle(1, b_rb, b_zs, b_zb),
        "b3": lambda: scan_late(1, b_rb, b_zb, b_pb, b_fb, True),
        "b4": lambda: scan_end(1, b_fb),
    }
    for b in range(BLOCKS):
        steps[f"mask{b}"] = functools.partial(mask, b)
        steps[f"send{b}"] = functools.partial(do_send, b)
        steps[f"relay{b}"] = functools.partial(do_relay, b)
        steps[f"add{b}"] = functools.partial(add_relayed, b)
        steps[f"local{b}"] = functools.partial(back_local, b, 0)
        steps[f"fin{b}"] = functools.partial(finish, b)
        steps[f"far{b}"] = functools.partial(do_far_mix, b)
    for j in range(4):
        steps[f"gn{j}"] = functools.partial(grad_normed, j)
        for n, act in enumerate((w_start, w_x, w_z, w_turn, w_x_back, w_core_back, w_end)):
            steps[f"w{n}_{j}"] = functools.partial(act, j)
    for name in ORDER:
        steps[name]()

    left(gp.at[pl.ds(0, 2)], ag_s.at[0])
    left(gp.at[3], ag_s.at[1])
    left(ps.at[2], rs_s.at[0])
    left(ps.at[pl.ds(0, 2)], rs_s.at[1])
    for n, (eight, zs) in enumerate(((f_rb, f_zb), (b_rb, b_zb))):
        left(eight.at[pl.ds(0, N_ROW - 1)], scan_s.at[n, 0])
        left(zs.at[pl.ds(0, N_Z - 1)], scan_s.at[n, 1])
        left(eight.at[pl.ds(0, N_ROW - 1)], scan_s.at[n, 2])
    left(wsend, w_s.at[0])
    left(xg, w_s.at[1])
    left(xs.at[:, pl.ds(0, N_X - 1)], w_s.at[2])
    left(xg.at[:, pl.ds(0, N_X - 1)], w_s.at[3])
    left(zsw.at[:, pl.ds(0, N_Z - 1)], w_s.at[4])
    left(zg.at[:, pl.ds(0, N_Z - 1)], w_s.at[5])


def write_out(*refs):
    sources, targets, done = refs[:5], refs[5:10], refs[10]
    for i, (source, target) in enumerate(zip(sources, targets)):
        part = source.shape[0] // 4
        for n in range(4):
            at = pl.ds(n * part, part)
            pltpu.make_async_copy(source.at[at], target.at[at], done.at[i]).start()
    for i, (source, target) in enumerate(zip(sources, targets)):
        pltpu.make_async_copy(source, target, done.at[i]).wait()


def local(queries, attn_keys, attn_values, out_weight, grad_out, drop_seed):
    square = (ROWS, WIDTH)
    vmem = pltpu.VMEM
    scan_buffers = [
        vmem((8, 64, 128), BF16),
        vmem((8, 64, 128), BF16),
        vmem((64, 128), BF16),
        vmem((8, 64, 128), BF16),
        vmem((8, 64, 128), BF16),
        vmem((8, 64, 128), BF16),
    ]
    dma = pltpu.SemaphoreType.DMA
    scratch = [
        vmem(square, BF16), vmem(square, BF16), vmem(square, BF16), vmem(square, BF16),
        vmem((WIDTH, MODEL), BF16),
        vmem(square, F32),
        vmem((4,) + square, BF16),
        vmem((BLOCKS, HEADS, HD, HD), F32),
        vmem((BLOCKS * HEADS, SPAN, SPAN), BF16),
        vmem((BLOCKS * HEADS, HD, HD), BF16),
        vmem(square, F32),
        vmem(square, F32),
        vmem(square, BF16),
        vmem((WIDTH, ROWS), BF16),
        vmem((3,) + square, BF16),
        vmem(square, F32),
        vmem((2, BLOCKS, HALF, WIDTH), BF16),
        vmem((2,) + square, BF16),
        vmem(square, F32),
        vmem(square, BF16),
        vmem((BLOCKS, HEADS, HD, HD), F32),
        vmem(square, F32), vmem(square, F32),
        *scan_buffers, *scan_buffers,
        pltpu.SMEM((1,), jnp.int32),
        vmem((4, 256, 512), BF16),
        vmem((4, 256, 512), F32),
        vmem((4, 256, 512), BF16),
        vmem((4, 4, 64, 512), BF16),
        vmem((4, 4, 64, 512), BF16),
        vmem((4, 8, 16, 256), BF16),
        vmem((4, 8, 16, 256), BF16),
        vmem((4, 16, 256), BF16),
        vmem((4, 8, 16, 256), BF16),
        vmem((4, 4, 64, 512), BF16),
        vmem((4, 4, 64, 512), BF16),
        dma((7,)),
        dma((2,)), dma((7,)),
        dma((2,)), dma((6,)),
        dma((2, 3)), dma((2, 3)),
        dma((6,)), dma((6, 4)),
    ]
    hbm = pl.BlockSpec(memory_space=pl.ANY)
    outs = pl.pallas_call(
        kernel,
        out_shape=[vmem(square, BF16)] * 4 + [vmem((8, 64, MODEL), BF16)],
        in_specs=[hbm] * 6,
        out_specs=[pl.BlockSpec(memory_space=vmem)] * 5,
        scratch_shapes=scratch,
        compiler_params=pltpu.CompilerParams(
            collective_id=0, has_side_effects=True, vmem_limit_bytes=56 * 1024 * 1024
        ),
        cost_estimate=pl.CostEstimate(
            flops=7_000_000_000, bytes_accessed=11_000_000, transcendentals=3072
        ),
        name="layer",
    )(drop_seed, queries, attn_keys, attn_values, out_weight, grad_out)
    output, grad_q, grad_k, grad_v, grad_w = pl.pallas_call(
        write_out,
        out_shape=[jax.ShapeDtypeStruct(square, BF16)] * 4
        + [jax.ShapeDtypeStruct((8, 64, MODEL), BF16)],
        in_specs=[pl.BlockSpec(memory_space=vmem)] * 5,
        out_specs=[hbm] * 5,
        scratch_shapes=[dma((5,))],
        compiler_params=pltpu.CompilerParams(vmem_limit_bytes=1024 * 1024),
        name="write_out",
    )(*outs)
    return output, grad_q, grad_k, grad_v, grad_w.reshape(WIDTH, MODEL)


def solution(mesh):
    tokens = P("seq", "head")
    weight = P("head", None)
    return jax.shard_map(
        local,
        mesh=mesh,
        in_specs=(tokens, tokens, tokens, weight, tokens, P()),
        out_specs=(tokens, tokens, tokens, tokens, weight),
        check_vma=False,
    )
```
